128 devices in a mesh: dp: 32 (over z, x, y_lo), pool: 4 (over y_hi, core).
Axes of the slice: x: 4, y: 4 (y_hi: 2, y_lo: 2; y = y_hi * 2 + y_lo), z: 4, core: 2. Of those that a mesh axis runs over, the one named last changes fastest.
Arguments:
- pool_image: bfloat16 [98304, 1152], P(('dp', 'pool')), may hold values from -0.23925781 to 0.23925781
- pool_text: bfloat16 [98304, 1152], P(('dp', 'pool')), may hold values from -0.23925781 to 0.23925781
- owners: int32 [32768, 1], P(('dp', 'pool')), may hold values from 0 to 127; in each aligned block of 256 rows (0 to 255, 256 to 511, ...) at most 4 rows name the same one
- slot_index: int32 [32768], P(('dp', 'pool')), may hold values from 0 to 767
Outputs:
- grad_image: float32 [32768, 1152], P(('dp', 'pool'))
- grad_text: float32 [32768, 1152], P(('dp', 'pool'))
The draws below stay inside these ranges and needn't reach their ends.
Inputs may be any that keep to these rules, and one draw needn't show every extreme that they name: `owners`: among the 256 rows of one device at most 4 name the same owner.
All inputs are finite; a program needn't handle non-finite values.
Results may differ from the reference program's by a relative error of at most 0.0042.
Values may be sent and summed in bfloat16 or wider, within the bound.
A program may use at most 64 MiB of HBM per device.

```python
import math
from functools import partial
import jax
import jax.numpy as jnp
import numpy as np
from jax import lax

EMBED = 1152
BLOCK = 256
CYCLE_STEPS = 2
POOL_DEV = 768
SUB = 32768
POOL = 98304
N_DP = 32
N_POOL = 4


def plant(result, rng, least, high):
    place = [jax.random.randint(jax.random.fold_in(rng, axis), (), 0, length) for axis, length in enumerate(result.shape)]
    main_axis = result.shape.index(max(result.shape))
    neighbour = place[:main_axis] + [(place[main_axis] + 1) % result.shape[main_axis]] + place[main_axis + 1:]
    return result.at[tuple(place)].set(least).at[tuple(neighbour)].set(high)


def steps_of(key, dims, split, least, largest):
    loudness = 1.0
    for position, blocks in split:
        steps = jax.random.uniform(jax.random.fold_in(jax.random.fold_in(key, 6), position), (blocks,), jnp.float32, least / len(split), largest / len(split))
        loudness = loudness * jnp.repeat(jnp.exp(steps), dims[position] // blocks).reshape((-1,) + (1,) * (len(dims) - 1 - position))
    return loudness


def shared_out(rng, own, number, rows, amount, top, bound, slope):
    sequence = jax.random.permutation(rng, amount)
    crowded, ordinary = shares(amount, rows * top, bound, slope, True), shares(amount, rows * top, bound, slope, False)
    places = jnp.arange(amount)

    def named(sizes, turn):
        used = int((sizes > 0).sum())
        fixed = max(1, used // 4)
        shifted = fixed + (places - fixed + turn * (used - fixed)) % max(1, amount - fixed)
        return jnp.zeros((amount,), jnp.int32).at[sequence[jnp.where(places < fixed, places, shifted)]].set(jnp.asarray(sizes, jnp.int32))

    sizes = jnp.where(number % 4 == 0, named(crowded, number // 4), named(ordinary, number - number // 4 - 1))
    mixed = jax.random.permutation(jax.random.fold_in(own, 3), amount)
    source_of, receiver = mixed[0:amount // 2 * 2:2], mixed[1:amount // 2 * 2:2]
    room = jnp.minimum(sizes[source_of] - 1, bound - sizes[receiver]) // 2
    room = jnp.where((source_of == sequence[0]) | (receiver == sequence[0]) | (sizes[receiver] == 0), 0, jnp.maximum(room, 0))
    shifted = jax.random.randint(jax.random.fold_in(own, 4), (amount // 2,), 0, 1 << 20) % (room + 1)
    sizes = sizes.at[source_of].add(-shifted).at[receiver].add(shifted)
    items = jnp.searchsorted(jnp.cumsum(sizes), jnp.arange(rows * top), side="right").astype(jnp.int32)
    grid = items.reshape(top, rows).T
    grid = grid[jax.random.permutation(jax.random.fold_in(own, 1), rows)]
    turn = jax.random.randint(jax.random.fold_in(own, 2), (rows, 1), 0, top)
    return jnp.take_along_axis(grid, (jnp.arange(top)[None, :] + turn) % top, axis=1)


def shares(number_of, total, reach, slope, full):
    weights = [(1 << 20) // math.isqrt(grade ** slope) + 1 for grade in range(1, number_of + 1)]
    largest = reach if full else min(reach, max(-(-total // number_of), total * weights[0] // sum(weights)))
    least = 1 if total - largest >= number_of - 1 else 0
    holding, surplus = [largest] + [least] * (number_of - 1), total - largest - least * (number_of - 1)
    while surplus > 0:
        free = [i for i in range(1, number_of) if holding[i] < largest] or [i for i in range(1, number_of) if holding[i] < reach]
        whole, left = sum([weights[i] for i in free]), surplus
        for i in free:
            addition = min(reach - holding[i], max(1, left * weights[i] // whole), surplus)
            holding[i] = holding[i] + addition
            surplus = surplus - addition
    return np.array(holding)


def gaussian(own_key, extent, deviation, reach, split=(), kind=jnp.bfloat16):
    array = jax.random.normal(own_key, extent, jnp.float32) * deviation
    if len(split) > 0:
        array = steps_of(own_key, extent, split, -0.22, 0.18) * array
    return jnp.clip(array, min=-reach, max=reach).astype(kind)


def setup_inputs(seed: int = 0) -> dict:
    splits = jax.random.split(jax.random.key(seed), 5)
    pool_image = gaussian(splits[0], (POOL, EMBED), 0.03, 0.23925781, ((0, 128),))
    pool_text = gaussian(splits[1], (POOL, EMBED), 0.03, 0.23925781, ((0, 128),))
    owners_keys = jax.random.split(jax.random.fold_in(splits[2], 1), SUB // BLOCK)
    owners_turns = jax.random.permutation(jax.random.fold_in(splits[2], 3), SUB // BLOCK)
    owners = jax.vmap(lambda own, number: shared_out(jax.random.fold_in(splits[2], 2), own, number, BLOCK, N_DP * N_POOL, 1, 2 * BLOCK // (N_DP * N_POOL), 2))(owners_keys, owners_turns).reshape((SUB, 1))
    slot_index = plant(jax.random.randint(splits[3], (SUB,), 0, POOL_DEV), jax.random.fold_in(splits[3], 1), 0, POOL_DEV - 1).astype(jnp.int32)
    return dict(pool_image=pool_image, pool_text=pool_text, owners=owners, slot_index=slot_index)


logit_scale = 10.0
logit_bias = -2.0
norm_eps = 1e-06

def normalize(values):
    widened = values.astype(jnp.float32)
    inverse = lax.rsqrt(lax.optimization_barrier(jnp.sum(widened * widened, axis=-1, keepdims=True)) + norm_eps)
    return (widened * inverse, inverse)

def unnormalize(unit_rows, inverse, upstream):
    return inverse * (upstream - unit_rows * lax.optimization_barrier(jnp.sum(unit_rows * upstream, axis=-1, keepdims=True)))

def pair_gradients(image_unit, text_unit, positive):
    logits = logit_scale * lax.dot_general(image_unit, text_unit, (((1,), (1,)), ((), ())), preferred_element_type=jnp.float32) + logit_bias
    row_count = logits.shape[0]
    labels = (lax.broadcasted_iota(jnp.int32, (row_count, row_count), 0) == lax.broadcasted_iota(jnp.int32, (row_count, row_count), 1)).astype(jnp.float32)
    weights = (jax.nn.sigmoid(logits) - positive * labels).astype(jnp.bfloat16)
    image_grad = logit_scale * jnp.dot(weights, text_unit, preferred_element_type=jnp.float32)
    text_grad = logit_scale * lax.dot_general(weights, image_unit, (((0,), (0,)), ((), ())), preferred_element_type=jnp.float32)
    return (image_grad, text_grad)

def paired(operands, positive):
    return pair_gradients(operands[0], operands[1], positive)

def reference(pool_image, pool_text, owners, slot_index):
    row_ids = (owners[:, 0] * POOL_DEV + slot_index).astype(jnp.int32)
    image_float, image_inverse = normalize(pool_image[row_ids])
    text_float, text_inverse = normalize(pool_text[row_ids])
    image_unit = image_float.astype(jnp.bfloat16)
    text_unit = text_float.astype(jnp.bfloat16)
    block_count = N_DP * N_POOL
    grid_shape = (N_DP, N_POOL, BLOCK, EMBED)
    image_blocks = image_unit.reshape(block_count, BLOCK, EMBED)
    text_grid = text_unit.reshape(grid_shape)
    image_total = jnp.zeros((block_count, BLOCK, EMBED), jnp.float32)
    text_total = jnp.zeros((block_count, BLOCK, EMBED), jnp.float32)
    for offset in range(CYCLE_STEPS + 1):
        partner = jnp.roll(text_grid, offset, axis=0).reshape(block_count, BLOCK, EMBED)
        positive = 1.0 if offset == 0 else 0.0
        image_part, text_part = lax.map(partial(paired, positive=positive), (image_blocks, partner))
        image_total = image_total + image_part
        text_total = text_total + jnp.roll(text_part.reshape(grid_shape), -offset, axis=0).reshape(block_count, BLOCK, EMBED)
    grad_image = unnormalize(image_float, image_inverse, image_total.reshape(-1, EMBED))
    grad_text = unnormalize(text_float, text_inverse, text_total.reshape(-1, EMBED))
    return (grad_image, grad_text)
```

```python
import functools
import jax
import jax.numpy as jnp
from jax import lax
from jax.experimental import pallas as pl
from jax.experimental.pallas import tpu as pltpu
from jax.sharding import PartitionSpec as P

EMBED = 1152
BLOCK = 256
POOL_DEV = 768
CHIPS = 64
SLOTS = 8
PARTS = ((0, 640), (640, 512))
MESH = pl.DeviceIdType.MESH
F32 = jnp.float32
BF16 = jnp.bfloat16

logit_scale = 10.0
logit_bias = -2.0
norm_eps = 1e-06


def dot(left, right):
    return lax.dot_general(left, right, (((1,), (0,)), ((), ())), preferred_element_type=F32)


def dot_t(left, right):
    return lax.dot_general(left, right, (((1,), (1,)), ((), ())), preferred_element_type=F32)


def iota(shape, axis):
    return lax.broadcasted_iota(jnp.int32, shape, axis)


def kernel(
    pool_image, pool_text, owners, slots,
    grad_image, grad_text,
    pools, requests, asked, picks, places, wide, out_a, out_b, back_a, back_b,
    raw, text_in, image_in, acc,
    local_sem, pool_send, pool_recv, ask_send, ask_recv, row_send, row_recv,
    ring_send, ring_recv, out_sem,
):
    a = lax.axis_index("dp")
    c = lax.axis_index("pool")
    z, x, y_lo = lax.div(a, 8), lax.rem(lax.div(a, 2), 4), lax.rem(a, 2)
    y_hi, core = lax.div(c, 2), lax.rem(c, 2)
    y = y_hi * 2 + y_lo
    chip = a * 2 + y_hi

    def partner(d):
        tz = lax.rem(z + lax.div(d, 16), 4)
        tx = lax.rem(x + lax.rem(lax.div(d, 4), 4), 4)
        ty = lax.rem(y + lax.rem(d, 4), 4)
        ta = tz * 8 + tx * 2 + lax.rem(ty, 2)
        t_hi = lax.div(ty, 2)
        return ta * 2 + t_hi, (ta, t_hi * 2 + core)

    barrier = pltpu.get_barrier_semaphore()
    sibling = (a, y_hi * 2 + 1 - core)
    pl.semaphore_signal(barrier, inc=1, device_id=sibling, device_id_type=MESH)

    def greet(d, carry):
        pl.semaphore_signal(barrier, inc=1, device_id=partner(d)[1], device_id_type=MESH)
        return carry

    lax.fori_loop(1, CHIPS, greet, 0)

    mine = pl.ds(pl.multiple_of(core * POOL_DEV, POOL_DEV), POOL_DEV)
    loads = []
    for t, source in enumerate((pool_text, pool_image)):
        loads.append(pltpu.make_async_copy(source, pools.at[t, mine], local_sem.at[t]))
        loads[-1].start()

    own_col = jnp.broadcast_to(owners[...], (BLOCK, BLOCK)).astype(F32)
    own_row = own_col.T
    same = own_col == own_row
    i0, i1 = iota((BLOCK, BLOCK), 0), iota((BLOCK, BLOCK), 1)
    rank_row = jnp.sum(jnp.where(same & (i0 < i1), 1.0, 0.0), axis=0, keepdims=True)
    rank_col = jnp.sum(jnp.where(same & (i1 < i0), 1.0, 0.0), axis=1, keepdims=True)
    place_row = (own_row[0:1] * 4.0 + rank_row).astype(jnp.int32)
    place_col = (own_col[:, 0:1] * 4.0 + rank_col).astype(jnp.int32)
    wanted = (slots[...] + POOL_DEV * lax.rem(lax.div(place_row, 4), 2)).astype(F32)
    hit = iota((CHIPS * SLOTS, BLOCK), 0) == place_row
    asking = jnp.sum(jnp.where(hit, wanted, 0.0), axis=1, keepdims=True)
    requests[...] = jnp.broadcast_to(asking, (CHIPS * SLOTS, 128)).reshape(CHIPS, SLOTS, 128)

    pl.semaphore_wait(barrier, CHIPS)
    swaps = []
    for t, source in enumerate((pool_text, pool_image)):
        swaps.append(
            pltpu.make_async_remote_copy(
                src_ref=source, dst_ref=pools.at[t, mine],
                send_sem=pool_send.at[t], recv_sem=pool_recv.at[t],
                device_id=sibling, device_id_type=MESH,
            )
        )

    def ask(d, carry):
        number, device = partner(d)
        pltpu.make_async_remote_copy(
            src_ref=requests.at[number], dst_ref=asked.at[chip],
            send_sem=ask_send, recv_sem=ask_recv,
            device_id=device, device_id_type=MESH,
        ).start()
        return carry

    lax.fori_loop(1, CHIPS, ask, 0)
    for swap in swaps:
        swap.start()
    asked[chip] = requests[chip]

    landing = lax.div(place_col, 8) * 16 + lax.rem(place_col, 8)
    columns = iota((BLOCK, CHIPS * 16), 1)
    for t in range(2):
        places[t * BLOCK:(t + 1) * BLOCK] = jnp.where(columns == landing + 8 * t, 1.0, 0.0).astype(BF16)

    others = pl.ds(0, CHIPS - 1)
    pltpu.make_async_copy(asked.at[others], asked.at[others], ask_recv).wait()
    questions = asked[...].reshape(CHIPS * SLOTS, 128)
    lane = iota((CHIPS * SLOTS, 128), 1).astype(F32)
    for j in range(2 * POOL_DEV // 128):
        picks[:, j * 128:(j + 1) * 128] = jnp.where(questions == lane + 128.0 * j, 1.0, 0.0).astype(BF16)

    for t in range(2):
        loads[t].wait()
        swaps[t].wait_recv()

    outs, backs = (out_a, out_b), (back_a, back_b)
    for p, (first, width) in enumerate(PARTS):
        for t in range(2):
            wide[t, :, 0:width] = dot(picks[...], pools[t, :, first:first + width])
        found = [wide[t, :, 0:width].reshape(CHIPS, SLOTS, width) for t in range(2)]
        outs[p][...] = jnp.concatenate(found, axis=1).astype(BF16)

        def answer(d, carry, p=p):
            number, device = partner(d)
            pltpu.make_async_remote_copy(
                src_ref=outs[p].at[number], dst_ref=backs[p].at[chip],
                send_sem=row_send.at[p], recv_sem=row_recv.at[p],
                device_id=device, device_id_type=MESH,
            ).start()
            return carry

        lax.fori_loop(1, CHIPS, answer, 0)
        backs[p][chip] = outs[p][chip]

    rings = []
    for p, (first, width) in enumerate(PARTS):
        pltpu.make_async_copy(backs[p].at[others], backs[p].at[others], row_recv.at[p]).wait()
        rows = dot(places[...], backs[p][...].reshape(CHIPS * 16, width))
        raw[:, first:first + width] = rows.astype(BF16)
        span = pl.ds(first, width)
        for k in (1, 2):
            for t, (buffer, step) in enumerate(((text_in, k), (image_in, 32 - k))):
                copy = pltpu.make_async_remote_copy(
                    src_ref=raw.at[pl.ds(t * BLOCK, BLOCK), span], dst_ref=buffer.at[k - 1, :, span],
                    send_sem=ring_send.at[p, k - 1, t], recv_sem=ring_recv.at[p, k - 1, t],
                    device_id=(lax.rem(a + step, 32), c), device_id_type=MESH,
                )
                copy.start()
                rings.append((p, k, t, copy))

    eye = i0 == i1

    def inverses(gram):
        kept = jnp.where(eye, gram, 0.0)
        return (
            lax.rsqrt(jnp.sum(kept, axis=1, keepdims=True) + norm_eps),
            lax.rsqrt(jnp.sum(kept, axis=0, keepdims=True) + norm_eps),
        )

    blocks = [raw[t * BLOCK:(t + 1) * BLOCK] for t in range(2)]
    own = [inverses(dot_t(block, block)) for block in blocks]

    def term(logits, col, row, positive):
        weights = 1.0 / (1.0 + jnp.exp(-(logit_scale * (logits * col * row) + logit_bias)))
        if positive:
            weights = weights - jnp.where(eye, 1.0, 0.0)
        return (weights * (logit_scale * row)).astype(BF16)

    for side in range(2):
        other = 1 - side
        weights = term(dot_t(blocks[side], blocks[other]), own[side][0], own[other][1], True)
        acc[side] = dot(weights, blocks[other])
    for k in (1, 2):
        for t in range(2):
            side = 1 - t
            for ring in rings:
                if ring[1] == k and ring[2] == t:
                    ring[3].wait_recv()
            block = (text_in, image_in)[t][k - 1]
            row = inverses(dot_t(block, block))[1]
            weights = term(dot_t(blocks[side], block), own[side][0], row, False)
            acc[side] += dot(weights, block)
    written = []
    for side, target in enumerate((grad_text, grad_image)):
        inverse = own[side][0]
        unit = blocks[side].astype(F32) * inverse
        total = acc[side]
        acc[side] = inverse * (total - unit * jnp.sum(unit * total, axis=-1, keepdims=True))
        written.append(pltpu.make_async_copy(acc.at[side], target, out_sem.at[side]))
        written[-1].start()

    pltpu.make_async_copy(requests.at[others], requests.at[others], ask_send).wait()
    for p in range(len(PARTS)):
        pltpu.make_async_copy(outs[p].at[others], outs[p].at[others], row_send.at[p]).wait()
    for t in range(2):
        swaps[t].wait_send()
    for ring in rings:
        ring[3].wait_send()
    for copy in written:
        copy.wait()


def shards(pool_image, pool_text, owners, slot_index):
    widths = [width for _, width in PARTS]
    gradient = jax.ShapeDtypeStruct((BLOCK, EMBED), F32)
    anywhere, vmem = pl.BlockSpec(memory_space=pl.ANY), pl.BlockSpec(memory_space=pltpu.VMEM)
    return tuple(pl.pallas_call(
        kernel,
        out_shape=(gradient, gradient),
        in_specs=[anywhere, anywhere, vmem, vmem],
        out_specs=(anywhere, anywhere),
        scratch_shapes=[
            pltpu.VMEM((2, 2 * POOL_DEV, EMBED), BF16),
            pltpu.VMEM((CHIPS, SLOTS, 128), F32),
            pltpu.VMEM((CHIPS, SLOTS, 128), F32),
            pltpu.VMEM((CHIPS * SLOTS, 2 * POOL_DEV), BF16),
            pltpu.VMEM((2 * BLOCK, CHIPS * 16), BF16),
            pltpu.VMEM((2, CHIPS * SLOTS, max(widths)), F32),
            *[pltpu.VMEM((CHIPS, 16, width), BF16) for width in widths],
            *[pltpu.VMEM((CHIPS, 16, width), BF16) for width in widths],
            pltpu.VMEM((2 * BLOCK, EMBED), BF16),
            pltpu.VMEM((2, BLOCK, EMBED), BF16),
            pltpu.VMEM((2, BLOCK, EMBED), BF16),
            pltpu.VMEM((2, BLOCK, EMBED), F32),
            pltpu.SemaphoreType.DMA((2,)),
            pltpu.SemaphoreType.DMA((2,)),
            pltpu.SemaphoreType.DMA((2,)),
            pltpu.SemaphoreType.DMA,
            pltpu.SemaphoreType.DMA,
            pltpu.SemaphoreType.DMA((len(PARTS),)),
            pltpu.SemaphoreType.DMA((len(PARTS),)),
            pltpu.SemaphoreType.DMA((len(PARTS), 2, 2)),
            pltpu.SemaphoreType.DMA((len(PARTS), 2, 2)),
            pltpu.SemaphoreType.DMA((2,)),
        ],
        compiler_params=pltpu.CompilerParams(
            collective_id=0, has_side_effects=True, vmem_limit_bytes=48 * 1024 * 1024
        ),
    )(pool_image, pool_text, owners, slot_index.reshape(1, BLOCK)))


def solution(mesh):
    in_specs = (
        P(("dp", "pool"), None),
        P(("dp", "pool"), None),
        P(("dp", "pool"), None),
        P(("dp", "pool")),
    )
    out_specs = (P(("dp", "pool"), None), P(("dp", "pool"), None))
    return jax.shard_map(shards, mesh=mesh, in_specs=in_specs, out_specs=out_specs, check_vma=False)
```

```python
import jax
import jax.numpy as jnp
from jax import lax
from jax.experimental import pallas as pl
from jax.experimental.pallas import tpu as pltpu
from jax.sharding import PartitionSpec as P

EMBED = 1152
BLOCK = 256
POOL_DEV = 768
CHIPS = 64
SLOTS = 8
PARTS = ((0, 384), (384, 384), (768, 384))
ROWS = 64
LIMIT_1 = 50
LIMIT_2 = 12
MESH = pl.DeviceIdType.MESH
F32 = jnp.float32
BF16 = jnp.bfloat16

logit_scale = 10.0
logit_bias = -2.0
norm_eps = 1e-06
OFFSETS = [(dz, dx, dy) for dx in range(4) for dy in range(4) for dz in range(4)][1:]


def dot(left, right):
    return lax.dot_general(left, right, (((1,), (0,)), ((), ())), preferred_element_type=F32)


def dot_t(left, right):
    return lax.dot_general(left, right, (((1,), (1,)), ((), ())), preferred_element_type=F32)


def iota(shape, axis):
    return lax.broadcasted_iota(jnp.int32, shape, axis)


def kernel(
    pool_image, pool_text, owners, slots,
    acc, raw,
    pools, requests, heard_1, heard_2, picks, places, wide, outs, backs,
    text_in, image_in,
    local_sem, pool_send, pool_recv, ask_send, ask_recv, row_send, row_recv,
    ring_send, ring_recv,
):
    a = lax.axis_index("dp")
    c = lax.axis_index("pool")
    z, x, y_lo = lax.div(a, 8), lax.rem(lax.div(a, 2), 4), lax.rem(a, 2)
    y_hi, core = lax.div(c, 2), lax.rem(c, 2)
    y = y_hi * 2 + y_lo
    to_z = [lax.rem(z + d, 4) for d in range(4)]
    to_x = [lax.rem(x + d, 4) for d in range(4)]
    to_y = [lax.rem(y + d, 4) for d in range(4)]
    to_lo = [lax.rem(t, 2) for t in to_y]
    to_hi = [lax.div(t, 2) for t in to_y]

    def first_half(dz, dy):
        return to_z[dz] * 2 + to_lo[dy]

    def second_half(dx, dy):
        return to_x[dx] * 2 + to_hi[dy]

    def device(dz, dx, dy):
        return to_z[dz] * 8 + to_x[dx] * 2 + to_lo[dy], to_hi[dy] * 2 + core

    def number(dz, dx, dy):
        return second_half(dx, dy) * 8 + first_half(dz, dy)

    chip = number(0, 0, 0)
    sibling = (a, y_hi * 2 + 1 - core)
    group_1 = [(to_z[d] * 2 + lo, (to_z[d] * 8 + x * 2 + lo, c)) for d in range(4) for lo in (y_lo, 1 - y_lo)][1:]
    group_2 = [(to_x[d] * 2 + hi, (z * 8 + to_x[d] * 2 + y_lo, hi * 2 + core)) for d in range(4) for hi in (y_hi, 1 - y_hi)][1:]
    me_1, me_2 = z * 2 + y_lo, x * 2 + y_hi

    barrier = pltpu.get_barrier_semaphore()
    greeted = [sibling] + [member[1] for member in group_1 + group_2]
    for peer in greeted:
        pl.semaphore_signal(barrier, inc=1, device_id=peer, device_id_type=MESH)

    mine = pl.ds(pl.multiple_of(core * POOL_DEV, POOL_DEV), POOL_DEV)
    loads = []
    for t, source in enumerate((pool_text, pool_image)):
        loads.append(pltpu.make_async_copy(source, pools.at[t, mine], local_sem.at[t]))
        loads[-1].start()

    i0, i1 = iota((BLOCK, BLOCK), 0), iota((BLOCK, BLOCK), 1)
    eye = i0 == i1
    own_row = jnp.broadcast_to(owners[...], (BLOCK, BLOCK)).astype(F32)
    slot_row = jnp.broadcast_to(slots[...], (BLOCK, BLOCK)).astype(F32)
    own_col = jnp.sum(jnp.where(eye, own_row, 0.0), axis=1, keepdims=True)
    slot_col = jnp.sum(jnp.where(eye, slot_row, 0.0), axis=1, keepdims=True)
    earlier = (own_col == own_row) & (i1 < i0)
    rank = jnp.sum(jnp.where(earlier, 1.0, 0.0), axis=1, keepdims=True).astype(jnp.int32)
    owner = own_col.astype(jnp.int32)
    o_1 = (owner >> 5) * 2 + ((owner >> 2) & 1)
    o_2 = ((owner >> 3) & 3) * 2 + ((owner >> 1) & 1)
    slot = (owner & 1) * 4 + rank
    wanted = slot_col + (POOL_DEV * (owner & 1)).astype(F32)
    lanes = iota((BLOCK, 128), 1)
    place = o_1 * 128 + o_2 * SLOTS + slot
    for t in range(8):
        requests[t] = jnp.sum(jnp.where(place == lanes + 128 * t, wanted, 0.0), axis=0, keepdims=True)

    pl.semaphore_wait(barrier, len(greeted))
    swaps = []
    for t, source in enumerate((pool_text, pool_image)):
        swaps.append(
            pltpu.make_async_remote_copy(
                src_ref=source, dst_ref=pools.at[t, mine],
                send_sem=pool_send.at[t], recv_sem=pool_recv.at[t],
                device_id=sibling, device_id_type=MESH,
            )
        )

    def tell(stage, group, source, target):
        copies = []
        for i, (to, peer) in enumerate(group):
            copies.append(pltpu.make_async_remote_copy(
                src_ref=source.at[to] if stage == 0 else source, dst_ref=target,
                send_sem=ask_send.at[stage, i], recv_sem=ask_recv.at[stage, i],
                device_id=peer, device_id_type=MESH,
            ))
            copies[-1].start()
        return copies

    asks = tell(0, group_1, requests, heard_1.at[me_1])
    for swap in swaps:
        swap.start()
    heard_1[me_1] = requests[me_1]

    landing = (o_2 * 8 + o_1) * 16 + slot
    columns = iota((BLOCK, CHIPS * 16), 1)
    for t in range(2):
        places[t * BLOCK:(t + 1) * BLOCK] = jnp.where(columns == landing + 8 * t, 1.0, 0.0).astype(BF16)

    for copy in asks:
        copy.wait_recv()
    later = tell(1, group_2, heard_1, heard_2.at[me_2])
    heard_2[me_2] = heard_1[...]
    for copy in later:
        copy.wait_recv()
    asks = asks + later
    others = pl.ds(0, CHIPS - 1)
    heard = jnp.broadcast_to(heard_2[...].reshape(CHIPS, 1, 128), (CHIPS, SLOTS, 128))
    here = iota((CHIPS, SLOTS, 128), 2) - iota((CHIPS, SLOTS, 128), 1) == me_2 * SLOTS
    questions = jnp.sum(jnp.where(here, heard, 0.0), axis=2, keepdims=True).reshape(CHIPS * SLOTS, 1)
    lane = iota((CHIPS * SLOTS, 128), 1).astype(F32)
    for j in range(2 * POOL_DEV // 128):
        picks[:, j * 128:(j + 1) * 128] = jnp.where(questions == lane + 128.0 * j, 1.0, 0.0).astype(BF16)

    for t in range(2):
        loads[t].wait()
        swaps[t].wait_recv()

    for p, (first, width) in enumerate(PARTS):
        for t in range(2):
            wide[t, :, 0:width] = dot(picks[...], pools[t, :, first:first + width])
        found = [wide[t, :, 0:width].reshape(CHIPS, SLOTS, width) for t in range(2)]
        outs[p][...] = jnp.concatenate(found, axis=1).astype(BF16)
        for offset in OFFSETS:
            pltpu.make_async_remote_copy(
                src_ref=outs[p].at[number(*offset)], dst_ref=backs[p].at[chip],
                send_sem=row_send.at[p], recv_sem=row_recv.at[p],
                device_id=device(*offset), device_id_type=MESH,
            ).start()
        backs[p][chip] = outs[p][chip]

    rings = {}
    for p, (first, width) in enumerate(PARTS):
        pltpu.make_async_copy(backs[p].at[others], backs[p].at[others], row_recv.at[p]).wait()
        rows = dot(places[...], backs[p][...].reshape(CHIPS * 16, width))
        raw[:, first:first + width] = rows.astype(BF16)
        span = pl.ds(first, width)
        for k in (2, 1):
            for t, (buffer, step) in enumerate(((text_in, k), (image_in, 32 - k))):
                copy = pltpu.make_async_remote_copy(
                    src_ref=raw.at[pl.ds(t * BLOCK, BLOCK), span], dst_ref=buffer.at[k - 1, :, span],
                    send_sem=ring_send.at[p, k - 1, t], recv_sem=ring_recv.at[p, k - 1, t],
                    device_id=(lax.rem(a + step, 32), c), device_id_type=MESH,
                )
                copy.start()
                rings[p, k, t] = copy

    def finish():
        for copy in asks:
            copy.wait_send()
        for p in range(len(PARTS)):
            pltpu.make_async_copy(outs[p].at[others], outs[p].at[others], row_send.at[p]).wait()
        for t in range(2):
            swaps[t].wait_send()
        for copy in rings.values():
            copy.wait_send()

    def inverses(gram):
        kept = jnp.where(eye, gram, 0.0)
        return (
            lax.rsqrt(jnp.sum(kept, axis=1, keepdims=True) + norm_eps),
            lax.rsqrt(jnp.sum(kept, axis=0, keepdims=True) + norm_eps),
        )

    blocks = [raw[t * BLOCK:(t + 1) * BLOCK] for t in range(2)]
    own = [inverses(dot_t(block, block)) for block in blocks]

    def term(logits, col, row, positive):
        weights = 1.0 / (1.0 + jnp.exp(-(logit_scale * (logits * col * row) + logit_bias)))
        if positive:
            weights = weights - jnp.where(eye, 1.0, 0.0)
        return (weights * (logit_scale * row)).astype(BF16)

    for side in range(2):
        other = 1 - side
        weights = term(dot_t(blocks[side], blocks[other]), own[side][0], own[other][1], True)
        acc[side] = dot(weights, blocks[other])
    for k, t in ((2, 0), (2, 1), (1, 0), (1, 1)):
        side = 1 - t
        for p in range(len(PARTS)):
            rings[p, k, t].wait_recv()
        block = (text_in, image_in)[t][k - 1]
        row = inverses(dot_t(block, block))[1]
        weights = term(dot_t(blocks[side], block), own[side][0], row, False)
        acc[side] += dot(weights, block)
    finish()


def unnormalize(total, raw, grad_text, grad_image, done, sem):
    copies = []
    for t, target in enumerate((grad_text, grad_image)):
        for i in range(0, BLOCK, ROWS):
            span = pl.ds(i, ROWS)
            rows = raw[pl.ds(t * BLOCK + i, ROWS)].astype(F32)
            inverse = lax.rsqrt(jnp.sum(rows * rows, axis=-1, keepdims=True) + norm_eps)
            unit = rows * inverse
            upstream = total[t, span]
            along = jnp.sum(unit * upstream, axis=-1, keepdims=True)
            done[t, span] = inverse * (upstream - unit * along)
            copies.append(pltpu.make_async_copy(done.at[t, span], target.at[span], sem.at[t, i // ROWS]))
            copies[-1].start()
    for copy in copies:
        copy.wait()


def shards(pool_image, pool_text, owners, slot_index):
    widths = [width for _, width in PARTS]
    hbm, vmem = pl.BlockSpec(memory_space=pltpu.HBM), pl.BlockSpec(memory_space=pltpu.VMEM)
    total, raw = pl.pallas_call(
        kernel,
        out_shape=(pltpu.VMEM((2, BLOCK, EMBED), F32), pltpu.VMEM((2 * BLOCK, EMBED), BF16)),
        in_specs=[hbm, hbm, vmem, vmem],
        out_specs=(vmem, vmem),
        scratch_shapes=[
            pltpu.VMEM((2, 2 * POOL_DEV, EMBED), BF16),
            pltpu.VMEM((8, 1, 128), F32),
            pltpu.VMEM((8, 1, 128), F32),
            pltpu.VMEM((8, 8, 1, 128), F32),
            pltpu.VMEM((CHIPS * SLOTS, 2 * POOL_DEV), BF16),
            pltpu.VMEM((2 * BLOCK, CHIPS * 16), BF16),
            pltpu.VMEM((2, CHIPS * SLOTS, max(widths)), F32),
            [pltpu.VMEM((CHIPS, 16, width), BF16) for width in widths],
            [pltpu.VMEM((CHIPS, 16, width), BF16) for width in widths],
            pltpu.VMEM((2, BLOCK, EMBED), BF16),
            pltpu.VMEM((2, BLOCK, EMBED), BF16),
            pltpu.SemaphoreType.DMA((2,)),
            pltpu.SemaphoreType.DMA((2,)),
            pltpu.SemaphoreType.DMA((2,)),
            pltpu.SemaphoreType.DMA((2, 7)),
            pltpu.SemaphoreType.DMA((2, 7)),
            pltpu.SemaphoreType.DMA((len(PARTS),)),
            pltpu.SemaphoreType.DMA((len(PARTS),)),
            pltpu.SemaphoreType.DMA((len(PARTS), 2, 2)),
            pltpu.SemaphoreType.DMA((len(PARTS), 2, 2)),
        ],
        compiler_params=pltpu.CompilerParams(
            collective_id=0, has_side_effects=True, vmem_limit_bytes=LIMIT_1 * 1024 * 1024
        ),
    )(*[
        pltpu.with_memory_space_constraint(operand, pltpu.HBM)
        for operand in (pool_image, pool_text, owners.reshape(1, BLOCK), slot_index.reshape(1, BLOCK))
    ])
    grad_text, grad_image = pl.pallas_call(
        unnormalize,
        out_shape=[jax.ShapeDtypeStruct((BLOCK, EMBED), F32)] * 2,
        in_specs=[vmem, vmem],
        out_specs=[pl.BlockSpec(memory_space=pltpu.HBM)] * 2,
        scratch_shapes=[
            pltpu.VMEM((2, BLOCK, EMBED), F32),
            pltpu.SemaphoreType.DMA((2, BLOCK // ROWS)),
        ],
        compiler_params=pltpu.CompilerParams(vmem_limit_bytes=LIMIT_2 * 1024 * 1024),
    )(total, raw)
    return grad_image, grad_text


def solution(mesh):
    in_specs = (
        P(("dp", "pool"), None),
        P(("dp", "pool"), None),
        P(("dp", "pool"), None),
        P(("dp", "pool")),
    )
    out_specs = (P(("dp", "pool"), None), P(("dp", "pool"), None))
    return jax.shard_map(shards, mesh=mesh, in_specs=in_specs, out_specs=out_specs, check_vma=False)
```

```python
import jax
import jax.numpy as jnp
from jax import lax
from jax.experimental import pallas as pl
from jax.experimental.pallas import tpu as pltpu
from jax.sharding import PartitionSpec as P

EMBED = 1152
BLOCK = 256
POOL_DEV = 768
CHIPS = 64
SLOTS = 8
PARTS = ((0, 256), (256, 384), (640, 512))
LAG = 2
ROWS = 64
LIMIT_1 = 50
LIMIT_2 = 12
MESH = pl.DeviceIdType.MESH
F32 = jnp.float32
BF16 = jnp.bfloat16

logit_scale = 10.0
logit_bias = -2.0
norm_eps = 1e-06
NEAR = [(dz, 0, fw, 0) for dz in range(4) for fw in range(2)][1:]
AWAY = [(0, dx, 0, fh) for dx in range(4) for fh in range(2)][1:]
FAR = [(dz, dx, fw, fh) for dx in range(4) for fh in range(2) for dz in range(4) for fw in range(2) if dx or fh]


def dot(left, right):
    return lax.dot_general(left, right, (((1,), (0,)), ((), ())), preferred_element_type=F32)


def dot_t(left, right):
    return lax.dot_general(left, right, (((1,), (1,)), ((), ())), preferred_element_type=F32)


def iota(shape, axis):
    return lax.broadcasted_iota(jnp.int32, shape, axis)


def kernel(
    pool_image, pool_text, owners, slots,
    acc, raw,
    pools, requests, heard_1, heard_2, early_picks, picks, places, early, outs, backs,
    others_in, units,
    local_sem, pool_send, pool_recv, ask_send, ask_recv, early_send, row_send, row_recv,
    ring_send, ring_recv,
):
    a = lax.axis_index("dp")
    c = lax.axis_index("pool")
    z, x, y_lo = lax.div(a, 8), lax.rem(lax.div(a, 2), 4), lax.rem(a, 2)
    y_hi, core = lax.div(c, 2), lax.rem(c, 2)
    w = lax.rem(y_lo + y_hi, 2)
    to_z = [lax.rem(z + d, 4) for d in range(4)]
    to_x = [lax.rem(x + d, 4) for d in range(4)]
    to_w, to_hi = (w, 1 - w), (y_hi, 1 - y_hi)
    to_lo = [[lax.rem(v + hi, 2) for hi in to_hi] for v in to_w]

    def first_half(way):
        return to_z[way[0]] * 2 + to_w[way[2]]

    def second_half(way):
        return to_x[way[1]] * 2 + to_hi[way[3]]

    def device(way):
        dz, dx, fw, fh = way
        return to_z[dz] * 8 + to_x[dx] * 2 + to_lo[fw][fh], to_hi[fh] * 2 + core

    def number(way):
        return second_half(way) * 8 + first_half(way)

    home = (0, 0, 0, 0)
    chip, me_1, me_2 = number(home), first_half(home), second_half(home)
    sibling = (a, y_hi * 2 + 1 - core)
    group_1 = [(first_half(way), device(way)) for way in NEAR]
    group_2 = [(second_half(way), device(way)) for way in AWAY]

    barrier = pltpu.get_barrier_semaphore()
    greeted = [sibling] + [member[1] for member in group_1 + group_2]
    for peer in greeted:
        pl.semaphore_signal(barrier, inc=1, device_id=peer, device_id_type=MESH)

    mine = pl.ds(pl.multiple_of(core * POOL_DEV, POOL_DEV), POOL_DEV)
    loads = []
    for t, source in enumerate((pool_text, pool_image)):
        loads.append(pltpu.make_async_copy(source, pools.at[t, mine], local_sem.at[t]))
        loads[-1].start()

    i0, i1 = iota((BLOCK, BLOCK), 0), iota((BLOCK, BLOCK), 1)
    eye = i0 == i1
    own_row = jnp.broadcast_to(owners[...], (BLOCK, BLOCK)).astype(F32)
    slot_row = jnp.broadcast_to(slots[...], (BLOCK, BLOCK)).astype(F32)
    own_col = jnp.sum(jnp.where(eye, own_row, 0.0), axis=1, keepdims=True)
    slot_col = jnp.sum(jnp.where(eye, slot_row, 0.0), axis=1, keepdims=True)
    earlier = (own_col == own_row) & (i1 < i0)
    rank = jnp.sum(jnp.where(earlier, 1.0, 0.0), axis=1, keepdims=True).astype(jnp.int32)
    owner = own_col.astype(jnp.int32)
    o_1 = (owner >> 5) * 2 + (((owner >> 2) + (owner >> 1)) & 1)
    o_2 = ((owner >> 3) & 3) * 2 + ((owner >> 1) & 1)
    slot = (owner & 1) * 4 + rank
    wanted = slot_col + (POOL_DEV * (owner & 1)).astype(F32)
    lanes = iota((BLOCK, 128), 1)
    place = o_1 * 128 + o_2 * SLOTS + slot
    for t in range(8):
        requests[t] = jnp.sum(jnp.where(place == lanes + 128 * t, wanted, 0.0), axis=0, keepdims=True)

    pl.semaphore_wait(barrier, len(greeted))
    swaps = []
    for p, (first, width) in enumerate(PARTS):
        span = pl.ds(first, width)
        for t, source in enumerate((pool_text, pool_image)):
            swaps.append(
                pltpu.make_async_remote_copy(
                    src_ref=source.at[:, span], dst_ref=pools.at[t, mine, span],
                    send_sem=pool_send.at[t, p], recv_sem=pool_recv.at[t, p],
                    device_id=sibling, device_id_type=MESH,
                )
            )

    def tell(stage, group, source, target):
        copies = []
        for i, (to, peer) in enumerate(group):
            copies.append(pltpu.make_async_remote_copy(
                src_ref=source.at[to] if stage == 0 else source, dst_ref=target,
                send_sem=ask_send.at[stage, i], recv_sem=ask_recv.at[stage, i],
                device_id=peer, device_id_type=MESH,
            ))
            copies[-1].start()
        return copies

    asks = tell(0, group_1, requests, heard_1.at[me_1])
    for swap in swaps:
        swap.start()
    heard_1[me_1] = requests[me_1]

    landing = (o_2 * 8 + o_1) * 16 + slot
    columns = iota((BLOCK, CHIPS * 16), 1)
    for t in range(2):
        places[t * BLOCK:(t + 1) * BLOCK] = jnp.where(columns == landing + 8 * t, 1.0, 0.0).astype(BF16)

    for copy in asks:
        copy.wait_recv()
    later = tell(1, group_2, heard_1, heard_2.at[me_2])
    heard_2[me_2] = heard_1[...]
    lane = iota((CHIPS * SLOTS, 128), 1).astype(F32)

    def pick(heard, chips, target):
        heard = jnp.broadcast_to(heard.reshape(chips, 1, 128), (chips, SLOTS, 128))
        here = iota(heard.shape, 2) - iota(heard.shape, 1) == me_2 * SLOTS
        questions = jnp.sum(jnp.where(here, heard, 0.0), axis=2, keepdims=True).reshape(chips * SLOTS, 1)
        for j in range(2 * POOL_DEV // 128):
            hits = questions == lane[:chips * SLOTS] + 128.0 * j
            target[:, j * 128:(j + 1) * 128] = jnp.where(hits, 1.0, 0.0).astype(BF16)

    def found(picked, chips, first, width):
        rows = [dot(picked[...], pools[t, :, first:first + width]) for t in range(2)]
        return jnp.concatenate([r.reshape(chips, SLOTS, width) for r in rows], axis=1).astype(BF16)

    def answer(source, p, way, sem):
        return pltpu.make_async_remote_copy(
            src_ref=source, dst_ref=backs[p].at[chip], send_sem=sem, recv_sem=row_recv.at[p],
            device_id=device(way), device_id_type=MESH,
        )

    pick(heard_1[...], 8, early_picks)
    for copy in loads:
        copy.wait()
    for p, (first, width) in enumerate(PARTS):
        for swap in swaps[2 * p:2 * p + 2]:
            swap.wait_recv()
        early[p][...] = found(early_picks, 8, first, width)
        for way in NEAR:
            answer(early[p].at[first_half(way)], p, way, early_send.at[p]).start()
        backs[p][chip] = early[p][me_1]

    for copy in later:
        copy.wait_recv()
    asks = asks + later
    others = pl.ds(0, CHIPS - 1)
    far = pl.ds(0, len(FAR))
    near = pl.ds(0, len(NEAR))
    pick(heard_2[...], CHIPS, picks)
    for p, (first, width) in enumerate(PARTS):
        outs[p][...] = found(picks, CHIPS, first, width)
        for way in FAR:
            answer(outs[p].at[number(way)], p, way, row_send.at[p]).start()

    odd = lax.rem(a, 2)
    neighbour = (a + 1 - 2 * odd, c)
    rings = {}

    def ring(p, role, source, target, peer):
        span = pl.ds(PARTS[p][0], PARTS[p][1])
        rings[p, role] = pltpu.make_async_remote_copy(
            src_ref=source.at[:, span], dst_ref=target.at[:, span],
            send_sem=ring_send.at[p, role], recv_sem=ring_recv.at[p, role],
            device_id=peer, device_id_type=MESH,
        )
        rings[p, role].start()

    def own_block(t):
        return raw.at[pl.ds(pl.multiple_of(t * BLOCK, BLOCK), BLOCK)]

    def pass_on(p):
        rings[p, 0].wait_recv()
        ring(p, 3, others_in.at[1 - odd, 1], others_in.at[1 - odd, 0], neighbour)

    for p, (first, width) in enumerate(PARTS):
        pltpu.make_async_copy(backs[p].at[others], backs[p].at[others], row_recv.at[p]).wait()
        rows = dot(places[...], backs[p][...].reshape(CHIPS * 16, width))
        raw[:, first:first + width] = rows.astype(BF16)
        for role, t in ((0, 1 - odd), (1, odd)):
            ring(p, role, own_block(t), others_in.at[t, 1], (lax.rem(a + 2 + 28 * t, 32), c))
        ring(p, 2, own_block(odd), others_in.at[odd, 0], neighbour)
        if p >= LAG:
            pass_on(p - LAG)
    for p in range(len(PARTS) - LAG, len(PARTS)):
        pass_on(p)

    def finish():
        for copy in asks:
            copy.wait_send()
        for p in range(len(PARTS)):
            pltpu.make_async_copy(outs[p].at[far], outs[p].at[far], row_send.at[p]).wait()
            pltpu.make_async_copy(early[p].at[near], early[p].at[near], early_send.at[p]).wait()
        for swap in swaps:
            swap.wait_send()
        for copy in rings.values():
            copy.wait_send()

    def normalized(block):
        rows = block.astype(F32)
        return (rows * lax.rsqrt(jnp.sum(rows * rows, axis=-1, keepdims=True) + norm_eps)).astype(BF16)

    def weights(left, right, positive):
        values = 1.0 / (1.0 + jnp.exp(-(logit_scale * dot_t(left, right) + logit_bias)))
        if positive:
            values = values - jnp.where(eye, 1.0, 0.0)
        return values.astype(BF16)

    for t in range(2):
        units[t] = normalized(raw[t * BLOCK:(t + 1) * BLOCK])
    for side in range(2):
        acc[side] = dot(weights(units[side], units[1 - side], True), units[1 - side])
    for role, t, k in ((0, 1 - odd, 2), (1, odd, 2), (2, 1 - odd, 1), (3, odd, 1)):
        if role:
            for p in range(len(PARTS)):
                rings[p, role].wait_recv()
        block = normalized(others_in[t, k - 1])
        acc[1 - t] += dot(weights(units[1 - t], block, False), block)
    finish()


def unnormalize(total, raw, grad_text, grad_image, done, sem):
    copies = []
    for t, target in enumerate((grad_text, grad_image)):
        for i in range(0, BLOCK, ROWS):
            span = pl.ds(i, ROWS)
            rows = raw[pl.ds(t * BLOCK + i, ROWS)].astype(F32)
            inverse = lax.rsqrt(jnp.sum(rows * rows, axis=-1, keepdims=True) + norm_eps)
            unit = rows * inverse
            upstream = logit_scale * total[t, span]
            along = jnp.sum(unit * upstream, axis=-1, keepdims=True)
            done[t, span] = inverse * (upstream - unit * along)
            copies.append(pltpu.make_async_copy(done.at[t, span], target.at[span], sem.at[t, i // ROWS]))
            copies[-1].start()
    for copy in copies:
        copy.wait()


def shards(pool_image, pool_text, owners, slot_index):
    widths = [width for _, width in PARTS]
    hbm, vmem = pl.BlockSpec(memory_space=pltpu.HBM), pl.BlockSpec(memory_space=pltpu.VMEM)
    total, raw = pl.pallas_call(
        kernel,
        out_shape=(pltpu.VMEM((2, BLOCK, EMBED), F32), pltpu.VMEM((2 * BLOCK, EMBED), BF16)),
        in_specs=[hbm, hbm, vmem, vmem],
        out_specs=(vmem, vmem),
        scratch_shapes=[
            pltpu.VMEM((2, 2 * POOL_DEV, EMBED), BF16),
            pltpu.VMEM((8, 1, 128), F32),
            pltpu.VMEM((8, 1, 128), F32),
            pltpu.VMEM((8, 8, 1, 128), F32),
            pltpu.VMEM((8 * SLOTS, 2 * POOL_DEV), BF16),
            pltpu.VMEM((CHIPS * SLOTS, 2 * POOL_DEV), BF16),
            pltpu.VMEM((2 * BLOCK, CHIPS * 16), BF16),
            [pltpu.VMEM((8, 16, width), BF16) for width in widths],
            [pltpu.VMEM((CHIPS, 16, width), BF16) for width in widths],
            [pltpu.VMEM((CHIPS, 16, width), BF16) for width in widths],
            pltpu.VMEM((2, 2, BLOCK, EMBED), BF16),
            pltpu.VMEM((2, BLOCK, EMBED), BF16),
            pltpu.SemaphoreType.DMA((2,)),
            pltpu.SemaphoreType.DMA((2, len(PARTS))),
            pltpu.SemaphoreType.DMA((2, len(PARTS))),
            pltpu.SemaphoreType.DMA((2, 7)),
            pltpu.SemaphoreType.DMA((2, 7)),
            pltpu.SemaphoreType.DMA((len(PARTS),)),
            pltpu.SemaphoreType.DMA((len(PARTS),)),
            pltpu.SemaphoreType.DMA((len(PARTS),)),
            pltpu.SemaphoreType.DMA((len(PARTS), 4)),
            pltpu.SemaphoreType.DMA((len(PARTS), 4)),
        ],
        compiler_params=pltpu.CompilerParams(
            collective_id=0, has_side_effects=True, vmem_limit_bytes=LIMIT_1 * 1024 * 1024
        ),
    )(*[
        pltpu.with_memory_space_constraint(operand, pltpu.HBM)
        for operand in (pool_image, pool_text, owners.reshape(1, BLOCK), slot_index.reshape(1, BLOCK))
    ])
    grad_text, grad_image = pl.pallas_call(
        unnormalize,
        out_shape=[jax.ShapeDtypeStruct((BLOCK, EMBED), F32)] * 2,
        in_specs=[vmem, vmem],
        out_specs=[pl.BlockSpec(memory_space=pltpu.HBM)] * 2,
        scratch_shapes=[
            pltpu.VMEM((2, BLOCK, EMBED), F32),
            pltpu.SemaphoreType.DMA((2, BLOCK // ROWS)),
        ],
        compiler_params=pltpu.CompilerParams(vmem_limit_bytes=LIMIT_2 * 1024 * 1024),
    )(total, raw)
    return grad_image, grad_text


def solution(mesh):
    in_specs = (
        P(("dp", "pool"), None),
        P(("dp", "pool"), None),
        P(("dp", "pool"), None),
        P(("dp", "pool")),
    )
    out_specs = (P(("dp", "pool"), None), P(("dp", "pool"), None))
    return jax.shard_map(shards, mesh=mesh, in_specs=in_specs, out_specs=out_specs, check_vma=False)
```

```python
import jax
import jax.numpy as jnp
from jax import lax
from jax.experimental import pallas as pl
from jax.experimental.pallas import tpu as pltpu
from jax.sharding import PartitionSpec as P

EMBED = 1152
BLOCK = 256
POOL_DEV = 768
CHIPS = 64
SLOTS = 8
PARTS = ((0, 256), (256, 512), (768, 384))
LAG = 2
ROWS = 64
LIMIT_1 = 50
LIMIT_2 = 12
MESH = pl.DeviceIdType.MESH
F32 = jnp.float32
BF16 = jnp.bfloat16

logit_scale = 10.0
logit_bias = -2.0
norm_eps = 1e-06
NEAR = [(dz, 0, fw, 0) for dz in range(4) for fw in range(2)][1:]
AWAY = [(0, dx, 0, fh) for dx in range(4) for fh in range(2)][1:]
FAR = [(dz, dx, fw, fh) for dx in range(4) for fh in range(2) for dz in range(4) for fw in range(2) if dx or fh]


def dot(left, right):
    return lax.dot_general(left, right, (((1,), (0,)), ((), ())), preferred_element_type=F32)


def dot_t(left, right):
    return lax.dot_general(left, right, (((1,), (1,)), ((), ())), preferred_element_type=F32)


def iota(shape, axis):
    return lax.broadcasted_iota(jnp.int32, shape, axis)


def unnormalized(block, total):
    rows = block.astype(F32)
    inverse = lax.rsqrt(jnp.sum(rows * rows, axis=-1, keepdims=True) + norm_eps)
    unit = rows * inverse
    upstream = logit_scale * total
    return inverse * (upstream - unit * jnp.sum(unit * upstream, axis=-1, keepdims=True))


def kernel(
    pool_image, pool_text, owners_at, slots_at,
    acc, raw,
    owners, slots, pools, requests, heard_1, heard_2, early_picks, picks, places, early, outs, backs,
    others_in, units,
    name_sem, local_sem, pool_send, pool_recv, ask_send, ask_recv, early_send, row_send, row_recv,
    ring_send, ring_recv,
):
    a = lax.axis_index("dp")
    c = lax.axis_index("pool")
    z, x, y_lo = lax.div(a, 8), lax.rem(lax.div(a, 2), 4), lax.rem(a, 2)
    y_hi, core = lax.div(c, 2), lax.rem(c, 2)
    w = lax.rem(y_lo + y_hi, 2)
    to_z = [lax.rem(z + d, 4) for d in range(4)]
    to_x = [lax.rem(x + d, 4) for d in range(4)]
    to_w, to_hi = (w, 1 - w), (y_hi, 1 - y_hi)
    to_lo = [[lax.rem(v + hi, 2) for hi in to_hi] for v in to_w]

    def first_half(way):
        return to_z[way[0]] * 2 + to_w[way[2]]

    def second_half(way):
        return to_x[way[1]] * 2 + to_hi[way[3]]

    def device(way):
        dz, dx, fw, fh = way
        return to_z[dz] * 8 + to_x[dx] * 2 + to_lo[fw][fh], to_hi[fh] * 2 + core

    def number(way):
        return second_half(way) * 8 + first_half(way)

    home = (0, 0, 0, 0)
    chip, me_1, me_2 = number(home), first_half(home), second_half(home)
    sibling = (a, y_hi * 2 + 1 - core)
    group_1 = [(first_half(way), device(way)) for way in NEAR]
    group_2 = [(second_half(way), device(way)) for way in AWAY]

    names = []
    for i, (source, target) in enumerate(((owners_at, owners), (slots_at, slots))):
        names.append(pltpu.make_async_copy(source, target, name_sem.at[i]))
        names[-1].start()
    barrier = pltpu.get_barrier_semaphore()
    greeted = [sibling] + [member[1] for member in group_1 + group_2]
    for peer in greeted:
        pl.semaphore_signal(barrier, inc=1, device_id=peer, device_id_type=MESH)

    mine = pl.ds(pl.multiple_of(core * POOL_DEV, POOL_DEV), POOL_DEV)
    loads = []
    for t, source in enumerate((pool_text, pool_image)):
        loads.append(pltpu.make_async_copy(source, pools.at[t, mine], local_sem.at[t]))
        loads[-1].start()

    for copy in names:
        copy.wait()
    i0, i1 = iota((BLOCK, BLOCK), 0), iota((BLOCK, BLOCK), 1)
    eye = i0 == i1
    own_row = jnp.broadcast_to(owners[...], (BLOCK, BLOCK)).astype(F32)
    slot_row = jnp.broadcast_to(slots[...], (BLOCK, BLOCK)).astype(F32)
    own_col = jnp.sum(jnp.where(eye, own_row, 0.0), axis=1, keepdims=True)
    slot_col = jnp.sum(jnp.where(eye, slot_row, 0.0), axis=1, keepdims=True)
    earlier = (own_col == own_row) & (i1 < i0)
    rank = jnp.sum(jnp.where(earlier, 1.0, 0.0), axis=1, keepdims=True).astype(jnp.int32)
    owner = own_col.astype(jnp.int32)
    o_1 = (owner >> 5) * 2 + (((owner >> 2) + (owner >> 1)) & 1)
    o_2 = ((owner >> 3) & 3) * 2 + ((owner >> 1) & 1)
    slot = (owner & 1) * 4 + rank
    wanted = slot_col + (POOL_DEV * (owner & 1)).astype(F32)
    lanes = iota((BLOCK, 128), 1)
    place = o_1 * 128 + o_2 * SLOTS + slot
    for t in range(8):
        requests[t] = jnp.sum(jnp.where(place == lanes + 128 * t, wanted, 0.0), axis=0, keepdims=True)

    pl.semaphore_wait(barrier, len(greeted))
    swaps = []
    for p, (first, width) in enumerate(PARTS):
        span = pl.ds(first, width)
        for t, source in enumerate((pool_text, pool_image)):
            swaps.append(
                pltpu.make_async_remote_copy(
                    src_ref=source.at[:, span], dst_ref=pools.at[t, mine, span],
                    send_sem=pool_send.at[t, p], recv_sem=pool_recv.at[t, p],
                    device_id=sibling, device_id_type=MESH,
                )
            )

    def tell(stage, group, source, target):
        copies = []
        for i, (to, peer) in enumerate(group):
            copies.append(pltpu.make_async_remote_copy(
                src_ref=source.at[to] if stage == 0 else source, dst_ref=target,
                send_sem=ask_send.at[stage, i], recv_sem=ask_recv.at[stage, i],
                device_id=peer, device_id_type=MESH,
            ))
            copies[-1].start()
        return copies

    asks = tell(0, group_1, requests, heard_1.at[me_1])
    for swap in swaps:
        swap.start()
    heard_1[me_1] = requests[me_1]

    landing = (o_2 * 8 + o_1) * 16 + slot
    columns = iota((BLOCK, CHIPS * 16), 1)
    for t in range(2):
        places[t * BLOCK:(t + 1) * BLOCK] = jnp.where(columns == landing + 8 * t, 1.0, 0.0).astype(BF16)

    for copy in asks:
        copy.wait_recv()
    later = tell(1, group_2, heard_1, heard_2.at[me_2])
    heard_2[me_2] = heard_1[...]
    lane = iota((CHIPS * SLOTS, 128), 1).astype(F32)

    def pick(heard, chips, target):
        heard = jnp.broadcast_to(heard.reshape(chips, 1, 128), (chips, SLOTS, 128))
        here = iota(heard.shape, 2) - iota(heard.shape, 1) == me_2 * SLOTS
        questions = jnp.sum(jnp.where(here, heard, 0.0), axis=2, keepdims=True).reshape(chips * SLOTS, 1)
        for j in range(2 * POOL_DEV // 128):
            hits = questions == lane[:chips * SLOTS] + 128.0 * j
            target[:, j * 128:(j + 1) * 128] = jnp.where(hits, 1.0, 0.0).astype(BF16)

    def found(picked, chips, first, width):
        rows = [dot(picked[...], pools[t, :, first:first + width]) for t in range(2)]
        return jnp.concatenate([r.reshape(chips, SLOTS, width) for r in rows], axis=1).astype(BF16)

    def answer(source, p, way, sem):
        return pltpu.make_async_remote_copy(
            src_ref=source, dst_ref=backs[p].at[chip], send_sem=sem, recv_sem=row_recv.at[p],
            device_id=device(way), device_id_type=MESH,
        )

    pick(heard_1[...], 8, early_picks)
    for copy in loads:
        copy.wait()
    for p, (first, width) in enumerate(PARTS):
        for swap in swaps[2 * p:2 * p + 2]:
            swap.wait_recv()
        early[p][...] = found(early_picks, 8, first, width)
        for way in NEAR:
            answer(early[p].at[first_half(way)], p, way, early_send.at[p]).start()
        backs[p][chip] = early[p][me_1]

    for copy in later:
        copy.wait_recv()
    asks = asks + later
    others = pl.ds(0, CHIPS - 1)
    far = pl.ds(0, len(FAR))
    near = pl.ds(0, len(NEAR))
    pick(heard_2[...], CHIPS, picks)
    for p, (first, width) in enumerate(PARTS):
        outs[p][...] = found(picks, CHIPS, first, width)
        for way in FAR:
            answer(outs[p].at[number(way)], p, way, row_send.at[p]).start()

    odd = lax.rem(a, 2)
    neighbour = (a + 1 - 2 * odd, c)
    rings = {}

    def ring(p, role, source, target, peer):
        span = pl.ds(PARTS[p][0], PARTS[p][1])
        rings[p, role] = pltpu.make_async_remote_copy(
            src_ref=source.at[:, span], dst_ref=target.at[:, span],
            send_sem=ring_send.at[p, role], recv_sem=ring_recv.at[p, role],
            device_id=peer, device_id_type=MESH,
        )
        rings[p, role].start()

    def own_block(t):
        return raw.at[pl.ds(pl.multiple_of(t * BLOCK, BLOCK), BLOCK)]

    def pass_on(p):
        rings[p, 0].wait_recv()
        ring(p, 3, others_in.at[1 - odd, 1], others_in.at[1 - odd, 0], neighbour)

    for p, (first, width) in enumerate(PARTS):
        pltpu.make_async_copy(backs[p].at[others], backs[p].at[others], row_recv.at[p]).wait()
        rows = dot(places[...], backs[p][...].reshape(CHIPS * 16, width))
        raw[:, first:first + width] = rows.astype(BF16)
        for role, t in ((0, 1 - odd), (1, odd)):
            ring(p, role, own_block(t), others_in.at[t, 1], (lax.rem(a + 2 + 28 * t, 32), c))
        ring(p, 2, own_block(odd), others_in.at[odd, 0], neighbour)
        if p >= LAG:
            pass_on(p - LAG)
    for p in range(len(PARTS) - LAG, len(PARTS)):
        pass_on(p)

    def finish():
        for copy in asks:
            copy.wait_send()
        for p in range(len(PARTS)):
            pltpu.make_async_copy(outs[p].at[far], outs[p].at[far], row_send.at[p]).wait()
            pltpu.make_async_copy(early[p].at[near], early[p].at[near], early_send.at[p]).wait()
        for swap in swaps:
            swap.wait_send()
        for copy in rings.values():
            copy.wait_send()

    def normalized(block):
        rows = block.astype(F32)
        return (rows * lax.rsqrt(jnp.sum(rows * rows, axis=-1, keepdims=True) + norm_eps)).astype(BF16)

    def weights(left, right, positive):
        values = 1.0 / (1.0 + jnp.exp(-(logit_scale * dot_t(left, right) + logit_bias)))
        if positive:
            values = values - jnp.where(eye, 1.0, 0.0)
        return values.astype(BF16)

    for t in range(2):
        units[t] = normalized(raw[t * BLOCK:(t + 1) * BLOCK])
    for side in range(2):
        acc[side] = dot(weights(units[side], units[1 - side], True), units[1 - side])
    for role, t, k in ((0, 1 - odd, 2), (1, odd, 2), (2, 1 - odd, 1), (3, odd, 1)):
        if role:
            for p in range(len(PARTS)):
                rings[p, role].wait_recv()
        block = normalized(others_in[t, k - 1])
        acc[1 - t] += dot(weights(units[1 - t], block, False), block)
        if role == 2:
            for i in range(0, BLOCK, ROWS):
                span = pl.ds(i, ROWS)
                at = pl.ds(pl.multiple_of(odd * BLOCK + i, ROWS), ROWS)
                acc[odd, span] = unnormalized(raw[at], acc[odd, span])
    finish()


def write(total, raw, grad_text, grad_image, done, sem):
    odd = lax.rem(lax.axis_index("dp"), 2)
    targets = (grad_text, grad_image)
    for side in range(2):

        @pl.when(odd == side)
        def _():
            whole = pltpu.make_async_copy(total.at[side], targets[side], sem.at[0])
            whole.start()
            copies = [whole]
            for i in range(0, BLOCK, ROWS):
                span = pl.ds(i, ROWS)
                done[span] = unnormalized(raw[pl.ds((1 - side) * BLOCK + i, ROWS)], total[1 - side, span])
                copies.append(pltpu.make_async_copy(done.at[span], targets[1 - side].at[span], sem.at[1 + i // ROWS]))
                copies[-1].start()
            for copy in copies:
                copy.wait()


def shards(pool_image, pool_text, owners, slot_index):
    widths = [width for _, width in PARTS]
    hbm, vmem = pl.BlockSpec(memory_space=pltpu.HBM), pl.BlockSpec(memory_space=pltpu.VMEM)
    total, raw = pl.pallas_call(
        kernel,
        out_shape=(pltpu.VMEM((2, BLOCK, EMBED), F32), pltpu.VMEM((2 * BLOCK, EMBED), BF16)),
        in_specs=[hbm] * 4,
        out_specs=(vmem, vmem),
        scratch_shapes=[
            pltpu.VMEM((1, BLOCK), jnp.int32),
            pltpu.VMEM((1, BLOCK), jnp.int32),
            pltpu.VMEM((2, 2 * POOL_DEV, EMBED), BF16),
            pltpu.VMEM((8, 1, 128), F32),
            pltpu.VMEM((8, 1, 128), F32),
            pltpu.VMEM((8, 8, 1, 128), F32),
            pltpu.VMEM((8 * SLOTS, 2 * POOL_DEV), BF16),
            pltpu.VMEM((CHIPS * SLOTS, 2 * POOL_DEV), BF16),
            pltpu.VMEM((2 * BLOCK, CHIPS * 16), BF16),
            [pltpu.VMEM((8, 16, width), BF16) for width in widths],
            [pltpu.VMEM((CHIPS, 16, width), BF16) for width in widths],
            [pltpu.VMEM((CHIPS, 16, width), BF16) for width in widths],
            pltpu.VMEM((2, 2, BLOCK, EMBED), BF16),
            pltpu.VMEM((2, BLOCK, EMBED), BF16),
            pltpu.SemaphoreType.DMA((2,)),
            pltpu.SemaphoreType.DMA((2,)),
            pltpu.SemaphoreType.DMA((2, len(PARTS))),
            pltpu.SemaphoreType.DMA((2, len(PARTS))),
            pltpu.SemaphoreType.DMA((2, 7)),
            pltpu.SemaphoreType.DMA((2, 7)),
            pltpu.SemaphoreType.DMA((len(PARTS),)),
            pltpu.SemaphoreType.DMA((len(PARTS),)),
            pltpu.SemaphoreType.DMA((len(PARTS),)),
            pltpu.SemaphoreType.DMA((len(PARTS), 4)),
            pltpu.SemaphoreType.DMA((len(PARTS), 4)),
        ],
        compiler_params=pltpu.CompilerParams(
            collective_id=0, has_side_effects=True, vmem_limit_bytes=LIMIT_1 * 1024 * 1024
        ),
    )(*[
        pltpu.with_memory_space_constraint(operand, pltpu.HBM)
        for operand in (pool_image, pool_text, owners.reshape(1, BLOCK), slot_index.reshape(1, BLOCK))
    ])
    grad_text, grad_image = pl.pallas_call(
        write,
        out_shape=[jax.ShapeDtypeStruct((BLOCK, EMBED), F32)] * 2,
        in_specs=[vmem, vmem],
        out_specs=[pl.BlockSpec(memory_space=pltpu.HBM)] * 2,
        scratch_shapes=[
            pltpu.VMEM((BLOCK, EMBED), F32),
            pltpu.SemaphoreType.DMA((1 + BLOCK // ROWS,)),
        ],
        compiler_params=pltpu.CompilerParams(vmem_limit_bytes=LIMIT_2 * 1024 * 1024),
    )(total, raw)
    return grad_image, grad_text


def solution(mesh):
    in_specs = (
        P(("dp", "pool"), None),
        P(("dp", "pool"), None),
        P(("dp", "pool"), None),
        P(("dp", "pool")),
    )
    out_specs = (P(("dp", "pool"), None), P(("dp", "pool"), None))
    return jax.shard_map(shards, mesh=mesh, in_specs=in_specs, out_specs=out_specs, check_vma=False)
```

```python
import jax
import jax.numpy as jnp
from jax import lax
from jax.experimental import pallas as pl
from jax.experimental.pallas import tpu as pltpu
from jax.sharding import PartitionSpec as P

EMBED = 1152
BLOCK = 256
POOL_DEV = 768
CHIPS = 64
SLOTS = 8
PARTS = ((0, 256), (256, 512), (768, 384))
LAG = 2
ROWS = 64
LIMIT_1 = 50
LIMIT_2 = 12
MESH = pl.DeviceIdType.MESH
F32 = jnp.float32
BF16 = jnp.bfloat16

logit_scale = 10.0
logit_bias = -2.0
norm_eps = 1e-06
NEAR = [(dz, 0, fw, 0) for dz in range(4) for fw in range(2)][1:]
AWAY = [(0, dx, 0, fh) for dx in range(4) for fh in range(2)][1:]
FAR = [(dz, dx, fw, fh) for dz in range(4) for fh in range(2) for dx in range(4) for fw in range(2) if dx or fh]


def dot(left, right):
    return lax.dot_general(left, right, (((1,), (0,)), ((), ())), preferred_element_type=F32)


def dot_t(left, right):
    return lax.dot_general(left, right, (((1,), (1,)), ((), ())), preferred_element_type=F32)


def iota(shape, axis):
    return lax.broadcasted_iota(jnp.int32, shape, axis)


def unnormalized(block, total):
    rows = block.astype(F32)
    inverse = lax.rsqrt(jnp.sum(rows * rows, axis=-1, keepdims=True) + norm_eps)
    unit = rows * inverse
    upstream = logit_scale * total
    return inverse * (upstream - unit * jnp.sum(unit * upstream, axis=-1, keepdims=True))


def kernel(
    pool_image, pool_text, owners_at, slots_at,
    acc, raw,
    owners, slots, pools, requests, heard_1, heard_2, early_picks, picks, places, early, outs, backs,
    others_in, units,
    name_sem, local_sem, pool_send, pool_recv, ask_send, ask_recv, early_send, row_send, row_recv,
    ring_send, ring_recv,
):
    a = lax.axis_index("dp")
    c = lax.axis_index("pool")
    z, x, y_lo = lax.div(a, 8), lax.rem(lax.div(a, 2), 4), lax.rem(a, 2)
    y_hi, core = lax.div(c, 2), lax.rem(c, 2)
    w = lax.rem(y_lo + y_hi, 2)
    to_z = [lax.rem(z + d, 4) for d in range(4)]
    to_x = [lax.rem(x + d, 4) for d in range(4)]
    to_w, to_hi = (w, 1 - w), (y_hi, 1 - y_hi)
    to_lo = [[lax.rem(v + hi, 2) for hi in to_hi] for v in to_w]

    def first_half(way):
        return to_z[way[0]] * 2 + to_w[way[2]]

    def second_half(way):
        return to_x[way[1]] * 2 + to_hi[way[3]]

    def device(way):
        dz, dx, fw, fh = way
        return to_z[dz] * 8 + to_x[dx] * 2 + to_lo[fw][fh], to_hi[fh] * 2 + core

    def number(way):
        return second_half(way) * 8 + first_half(way)

    home = (0, 0, 0, 0)
    chip, me_1, me_2 = number(home), first_half(home), second_half(home)
    sibling = (a, y_hi * 2 + 1 - core)
    group_1 = [(first_half(way), device(way)) for way in NEAR]
    group_2 = [(second_half(way), device(way)) for way in AWAY]

    names = []
    for i, (source, target) in enumerate(((owners_at, owners), (slots_at, slots))):
        names.append(pltpu.make_async_copy(source, target, name_sem.at[i]))
        names[-1].start()
    barrier = pltpu.get_barrier_semaphore()
    greeted = [sibling] + [member[1] for member in group_1 + group_2]
    for peer in greeted:
        pl.semaphore_signal(barrier, inc=1, device_id=peer, device_id_type=MESH)

    mine = pl.ds(pl.multiple_of(core * POOL_DEV, POOL_DEV), POOL_DEV)
    loads = []
    for t, source in enumerate((pool_text, pool_image)):
        loads.append(pltpu.make_async_copy(source, pools.at[t, mine], local_sem.at[t]))
        loads[-1].start()

    for copy in names:
        copy.wait()
    i0, i1 = iota((BLOCK, BLOCK), 0), iota((BLOCK, BLOCK), 1)
    eye = i0 == i1
    own_row = jnp.broadcast_to(owners[...], (BLOCK, BLOCK)).astype(F32)
    slot_row = jnp.broadcast_to(slots[...], (BLOCK, BLOCK)).astype(F32)
    own_col = jnp.sum(jnp.where(eye, own_row, 0.0), axis=1, keepdims=True)
    slot_col = jnp.sum(jnp.where(eye, slot_row, 0.0), axis=1, keepdims=True)
    earlier = (own_col == own_row) & (i1 < i0)
    rank = jnp.sum(jnp.where(earlier, 1.0, 0.0), axis=1, keepdims=True).astype(jnp.int32)
    owner = own_col.astype(jnp.int32)
    o_1 = (owner >> 5) * 2 + (((owner >> 2) + (owner >> 1)) & 1)
    o_2 = ((owner >> 3) & 3) * 2 + ((owner >> 1) & 1)
    slot = (owner & 1) * 4 + rank
    wanted = slot_col + (POOL_DEV * (owner & 1)).astype(F32)
    lanes = iota((BLOCK, 128), 1)
    place = o_1 * 128 + o_2 * SLOTS + slot
    for t in range(8):
        requests[t] = jnp.sum(jnp.where(place == lanes + 128 * t, wanted, 0.0), axis=0, keepdims=True)

    pl.semaphore_wait(barrier, len(greeted))
    swaps = []
    for p, (first, width) in enumerate(PARTS):
        span = pl.ds(first, width)
        for t, source in enumerate((pool_text, pool_image)):
            swaps.append(
                pltpu.make_async_remote_copy(
                    src_ref=source.at[:, span], dst_ref=pools.at[t, mine, span],
                    send_sem=pool_send.at[t, p], recv_sem=pool_recv.at[t, p],
                    device_id=sibling, device_id_type=MESH,
                )
            )

    def tell(stage, group, source, target):
        copies = []
        for i, (to, peer) in enumerate(group):
            copies.append(pltpu.make_async_remote_copy(
                src_ref=source.at[to] if stage == 0 else source, dst_ref=target,
                send_sem=ask_send.at[stage, i], recv_sem=ask_recv.at[stage, i],
                device_id=peer, device_id_type=MESH,
            ))
            copies[-1].start()
        return copies

    asks = tell(0, group_1, requests, heard_1.at[me_1])
    for swap in swaps:
        swap.start()
    heard_1[me_1] = requests[me_1]

    landing = (o_2 * 8 + o_1) * 16 + slot
    columns = iota((BLOCK, CHIPS * 16), 1)
    for t in range(2):
        places[t * BLOCK:(t + 1) * BLOCK] = jnp.where(columns == landing + 8 * t, 1.0, 0.0).astype(BF16)

    for copy in asks:
        copy.wait_recv()
    later = tell(1, group_2, heard_1, heard_2.at[me_2])
    heard_2[me_2] = heard_1[...]
    lane = iota((CHIPS * SLOTS, 128), 1).astype(F32)

    def pick(heard, chips, target):
        heard = jnp.broadcast_to(heard.reshape(chips, 1, 128), (chips, SLOTS, 128))
        here = iota(heard.shape, 2) - iota(heard.shape, 1) == me_2 * SLOTS
        questions = jnp.sum(jnp.where(here, heard, 0.0), axis=2, keepdims=True).reshape(chips * SLOTS, 1)
        for j in range(2 * POOL_DEV // 128):
            hits = questions == lane[:chips * SLOTS] + 128.0 * j
            target[:, j * 128:(j + 1) * 128] = jnp.where(hits, 1.0, 0.0).astype(BF16)

    def found(picked, chips, first, width):
        rows = [dot(picked[...], pools[t, :, first:first + width]) for t in range(2)]
        return jnp.concatenate([r.reshape(chips, SLOTS, width) for r in rows], axis=1).astype(BF16)

    def answer(source, p, way, sem):
        return pltpu.make_async_remote_copy(
            src_ref=source, dst_ref=backs[p].at[chip], send_sem=sem, recv_sem=row_recv.at[p],
            device_id=device(way), device_id_type=MESH,
        )

    pick(heard_1[...], 8, early_picks)
    for copy in loads:
        copy.wait()
    for p, (first, width) in enumerate(PARTS):
        for swap in swaps[2 * p:2 * p + 2]:
            swap.wait_recv()
        early[p][...] = found(early_picks, 8, first, width)
        for way in NEAR:
            answer(early[p].at[first_half(way)], p, way, early_send.at[p]).start()
        backs[p][chip] = early[p][me_1]

    for copy in later:
        copy.wait_recv()
    asks = asks + later
    others = pl.ds(0, CHIPS - 1)
    far = pl.ds(0, len(FAR))
    near = pl.ds(0, len(NEAR))
    pick(heard_2[...], CHIPS, picks)
    for p, (first, width) in enumerate(PARTS):
        outs[p][...] = found(picks, CHIPS, first, width)
        for way in FAR:
            answer(outs[p].at[number(way)], p, way, row_send.at[p]).start()

    odd = lax.rem(a, 2)
    neighbour = (a + 1 - 2 * odd, c)
    rings = {}

    def ring(p, role, source, target, peer):
        span = pl.ds(PARTS[p][0], PARTS[p][1])
        rings[p, role] = pltpu.make_async_remote_copy(
            src_ref=source.at[:, span], dst_ref=target.at[:, span],
            send_sem=ring_send.at[p, role], recv_sem=ring_recv.at[p, role],
            device_id=peer, device_id_type=MESH,
        )
        rings[p, role].start()

    def own_block(t):
        return raw.at[pl.ds(pl.multiple_of(t * BLOCK, BLOCK), BLOCK)]

    def pass_on(p):
        rings[p, 0].wait_recv()
        ring(p, 3, others_in.at[1 - odd, 1], others_in.at[1 - odd, 0], neighbour)

    for p, (first, width) in enumerate(PARTS):
        pltpu.make_async_copy(backs[p].at[others], backs[p].at[others], row_recv.at[p]).wait()
        rows = dot(places[...], backs[p][...].reshape(CHIPS * 16, width))
        raw[:, first:first + width] = rows.astype(BF16)
        for role, t in ((0, 1 - odd), (1, odd)):
            ring(p, role, own_block(t), others_in.at[t, 1], (lax.rem(a + 2 + 28 * t, 32), c))
        ring(p, 2, own_block(odd), others_in.at[odd, 0], neighbour)
        if p >= LAG:
            pass_on(p - LAG)
    for p in range(len(PARTS) - LAG, len(PARTS)):
        pass_on(p)

    def finish():
        for copy in asks:
            copy.wait_send()
        for p in range(len(PARTS)):
            pltpu.make_async_copy(outs[p].at[far], outs[p].at[far], row_send.at[p]).wait()
            pltpu.make_async_copy(early[p].at[near], early[p].at[near], early_send.at[p]).wait()
        for swap in swaps:
            swap.wait_send()
        for copy in rings.values():
            copy.wait_send()

    def normalized(block):
        rows = block.astype(F32)
        return (rows * lax.rsqrt(jnp.sum(rows * rows, axis=-1, keepdims=True) + norm_eps)).astype(BF16)

    def weights(left, right, positive):
        values = 1.0 / (1.0 + jnp.exp(-(logit_scale * dot_t(left, right) + logit_bias)))
        if positive:
            values = values - jnp.where(eye, 1.0, 0.0)
        return values.astype(BF16)

    for t in range(2):
        units[t] = normalized(raw[t * BLOCK:(t + 1) * BLOCK])
    for side in range(2):
        acc[side] = dot(weights(units[side], units[1 - side], True), units[1 - side])
    for role, t, k in ((0, 1 - odd, 2), (1, odd, 2), (2, 1 - odd, 1), (3, odd, 1)):
        if role:
            for p in range(len(PARTS)):
                rings[p, role].wait_recv()
        block = normalized(others_in[t, k - 1])
        acc[1 - t] += dot(weights(units[1 - t], block, False), block)
        if role == 2:
            for i in range(0, BLOCK, ROWS):
                span = pl.ds(i, ROWS)
                at = pl.ds(pl.multiple_of(odd * BLOCK + i, ROWS), ROWS)
                acc[odd, span] = unnormalized(raw[at], acc[odd, span])
    finish()


def write(total, raw, grad_text, grad_image, done, sem):
    odd = lax.rem(lax.axis_index("dp"), 2)
    targets = (grad_text, grad_image)
    for side in range(2):

        @pl.when(odd == side)
        def _():
            whole = pltpu.make_async_copy(total.at[side], targets[side], sem.at[0])
            whole.start()
            copies = [whole]
            for i in range(0, BLOCK, ROWS):
                span = pl.ds(i, ROWS)
                done[span] = unnormalized(raw[pl.ds((1 - side) * BLOCK + i, ROWS)], total[1 - side, span])
                copies.append(pltpu.make_async_copy(done.at[span], targets[1 - side].at[span], sem.at[1 + i // ROWS]))
                copies[-1].start()
            for copy in copies:
                copy.wait()


def shards(pool_image, pool_text, owners, slot_index):
    widths = [width for _, width in PARTS]
    hbm, vmem = pl.BlockSpec(memory_space=pltpu.HBM), pl.BlockSpec(memory_space=pltpu.VMEM)
    total, raw = pl.pallas_call(
        kernel,
        out_shape=(pltpu.VMEM((2, BLOCK, EMBED), F32), pltpu.VMEM((2 * BLOCK, EMBED), BF16)),
        in_specs=[hbm] * 4,
        out_specs=(vmem, vmem),
        scratch_shapes=[
            pltpu.VMEM((1, BLOCK), jnp.int32),
            pltpu.VMEM((1, BLOCK), jnp.int32),
            pltpu.VMEM((2, 2 * POOL_DEV, EMBED), BF16),
            pltpu.VMEM((8, 1, 128), F32),
            pltpu.VMEM((8, 1, 128), F32),
            pltpu.VMEM((8, 8, 1, 128), F32),
            pltpu.VMEM((8 * SLOTS, 2 * POOL_DEV), BF16),
            pltpu.VMEM((CHIPS * SLOTS, 2 * POOL_DEV), BF16),
            pltpu.VMEM((2 * BLOCK, CHIPS * 16), BF16),
            [pltpu.VMEM((8, 16, width), BF16) for width in widths],
            [pltpu.VMEM((CHIPS, 16, width), BF16) for width in widths],
            [pltpu.VMEM((CHIPS, 16, width), BF16) for width in widths],
            pltpu.VMEM((2, 2, BLOCK, EMBED), BF16),
            pltpu.VMEM((2, BLOCK, EMBED), BF16),
            pltpu.SemaphoreType.DMA((2,)),
            pltpu.SemaphoreType.DMA((2,)),
            pltpu.SemaphoreType.DMA((2, len(PARTS))),
            pltpu.SemaphoreType.DMA((2, len(PARTS))),
            pltpu.SemaphoreType.DMA((2, 7)),
            pltpu.SemaphoreType.DMA((2, 7)),
            pltpu.SemaphoreType.DMA((len(PARTS),)),
            pltpu.SemaphoreType.DMA((len(PARTS),)),
            pltpu.SemaphoreType.DMA((len(PARTS),)),
            pltpu.SemaphoreType.DMA((len(PARTS), 4)),
            pltpu.SemaphoreType.DMA((len(PARTS), 4)),
        ],
        compiler_params=pltpu.CompilerParams(
            collective_id=0, has_side_effects=True, vmem_limit_bytes=LIMIT_1 * 1024 * 1024
        ),
    )(*[
        pltpu.with_memory_space_constraint(operand, pltpu.HBM)
        for operand in (pool_image, pool_text, owners.reshape(1, BLOCK), slot_index.reshape(1, BLOCK))
    ])
    grad_text, grad_image = pl.pallas_call(
        write,
        out_shape=[jax.ShapeDtypeStruct((BLOCK, EMBED), F32)] * 2,
        in_specs=[vmem, vmem],
        out_specs=[pl.BlockSpec(memory_space=pltpu.HBM)] * 2,
        scratch_shapes=[
            pltpu.VMEM((BLOCK, EMBED), F32),
            pltpu.SemaphoreType.DMA((1 + BLOCK // ROWS,)),
        ],
        compiler_params=pltpu.CompilerParams(vmem_limit_bytes=LIMIT_2 * 1024 * 1024),
    )(total, raw)
    return grad_image, grad_text


def solution(mesh):
    in_specs = (
        P(("dp", "pool"), None),
        P(("dp", "pool"), None),
        P(("dp", "pool"), None),
        P(("dp", "pool")),
    )
    out_specs = (P(("dp", "pool"), None), P(("dp", "pool"), None))
    return jax.shard_map(shards, mesh=mesh, in_specs=in_specs, out_specs=out_specs, check_vma=False)
```

```python
import jax
import jax.numpy as jnp
from jax import lax
from jax.experimental import pallas as pl
from jax.experimental.pallas import tpu as pltpu
from jax.sharding import PartitionSpec as P

EMBED = 1152
BLOCK = 256
POOL_DEV = 768
CHIPS = 64
SLOTS = 8
PARTS = ((0, 256), (256, 512), (768, 384))
LAG = 2
ROWS = 32
LIMIT_1 = 50
LIMIT_2 = 12
MESH = pl.DeviceIdType.MESH
F32 = jnp.float32
BF16 = jnp.bfloat16

logit_scale = 10.0
logit_bias = -2.0
norm_eps = 1e-06
NEAR = [(dz, 0, fw, 0) for dz in range(4) for fw in range(2)][1:]
AWAY = [(0, dx, 0, fh) for dx in range(4) for fh in range(2)][1:]
FAR = [(dz, dx, fw, fh) for dz in range(4) for fh in range(2) for dx in range(4) for fw in range(2) if dx or fh]


def dot(left, right):
    return lax.dot_general(left, right, (((1,), (0,)), ((), ())), preferred_element_type=F32)


def dot_t(left, right):
    return lax.dot_general(left, right, (((1,), (1,)), ((), ())), preferred_element_type=F32)


def iota(shape, axis):
    return lax.broadcasted_iota(jnp.int32, shape, axis)


def unnormalized(block, total):
    rows = block.astype(F32)
    inverse = lax.rsqrt(jnp.sum(rows * rows, axis=-1, keepdims=True) + norm_eps)
    unit = rows * inverse
    upstream = logit_scale * total
    return inverse * (upstream - unit * jnp.sum(unit * upstream, axis=-1, keepdims=True))


def kernel(
    pool_image, pool_text, owners_at, slots_at,
    acc, raw,
    owners, slots, pools, requests, heard_1, heard_2, early_picks, picks, places, early, outs, backs,
    others_in, units,
    name_sem, local_sem, pool_send, pool_recv, ask_send, ask_recv, early_send, row_send, row_recv,
    ring_send, ring_recv,
):
    a = lax.axis_index("dp")
    c = lax.axis_index("pool")
    z, x, y_lo = lax.div(a, 8), lax.rem(lax.div(a, 2), 4), lax.rem(a, 2)
    y_hi, core = lax.div(c, 2), lax.rem(c, 2)
    w = lax.rem(y_lo + y_hi, 2)
    to_z = [lax.rem(z + d, 4) for d in range(4)]
    to_x = [lax.rem(x + d, 4) for d in range(4)]
    to_w, to_hi = (w, 1 - w), (y_hi, 1 - y_hi)
    to_lo = [[lax.rem(v + hi, 2) for hi in to_hi] for v in to_w]

    def first_half(way):
        return to_z[way[0]] * 2 + to_w[way[2]]

    def second_half(way):
        return to_x[way[1]] * 2 + to_hi[way[3]]

    def device(way):
        dz, dx, fw, fh = way
        return to_z[dz] * 8 + to_x[dx] * 2 + to_lo[fw][fh], to_hi[fh] * 2 + core

    def number(way):
        return second_half(way) * 8 + first_half(way)

    home = (0, 0, 0, 0)
    chip, me_1, me_2 = number(home), first_half(home), second_half(home)
    sibling = (a, y_hi * 2 + 1 - core)
    group_1 = [(first_half(way), device(way)) for way in NEAR]
    group_2 = [(second_half(way), device(way)) for way in AWAY]

    names = []
    for i, (source, target) in enumerate(((owners_at, owners), (slots_at, slots))):
        names.append(pltpu.make_async_copy(source, target, name_sem.at[i]))
        names[-1].start()
    barrier = pltpu.get_barrier_semaphore()
    greeted = [sibling] + [member[1] for member in group_1 + group_2]
    for peer in greeted:
        pl.semaphore_signal(barrier, inc=1, device_id=peer, device_id_type=MESH)

    mine = pl.ds(pl.multiple_of(core * POOL_DEV, POOL_DEV), POOL_DEV)
    loads = []
    for t, source in enumerate((pool_text, pool_image)):
        loads.append(pltpu.make_async_copy(source, pools.at[t, mine], local_sem.at[t]))
        loads[-1].start()

    for copy in names:
        copy.wait()
    i0, i1 = iota((BLOCK, BLOCK), 0), iota((BLOCK, BLOCK), 1)
    eye = i0 == i1
    own_row = jnp.broadcast_to(owners[...], (BLOCK, BLOCK)).astype(F32)
    slot_row = jnp.broadcast_to(slots[...], (BLOCK, BLOCK)).astype(F32)
    own_col = jnp.sum(jnp.where(eye, own_row, 0.0), axis=1, keepdims=True)
    slot_col = jnp.sum(jnp.where(eye, slot_row, 0.0), axis=1, keepdims=True)
    earlier = (own_col == own_row) & (i1 < i0)
    rank = jnp.sum(jnp.where(earlier, 1.0, 0.0), axis=1, keepdims=True).astype(jnp.int32)
    owner = own_col.astype(jnp.int32)
    o_1 = (owner >> 5) * 2 + (((owner >> 2) + (owner >> 1)) & 1)
    o_2 = ((owner >> 3) & 3) * 2 + ((owner >> 1) & 1)
    slot = (owner & 1) * 4 + rank
    wanted = slot_col + (POOL_DEV * (owner & 1)).astype(F32)
    lanes = iota((BLOCK, 128), 1)
    place = o_1 * 128 + o_2 * SLOTS + slot
    for t in range(8):
        requests[t] = jnp.sum(jnp.where(place == lanes + 128 * t, wanted, 0.0), axis=0, keepdims=True)

    pl.semaphore_wait(barrier, len(greeted))
    swaps = []
    for p, (first, width) in enumerate(PARTS):
        span = pl.ds(first, width)
        for t, source in enumerate((pool_text, pool_image)):
            swaps.append(
                pltpu.make_async_remote_copy(
                    src_ref=source.at[:, span], dst_ref=pools.at[t, mine, span],
                    send_sem=pool_send.at[t, p], recv_sem=pool_recv.at[t, p],
                    device_id=sibling, device_id_type=MESH,
                )
            )

    def tell(stage, group, source, target):
        copies = []
        for i, (to, peer) in enumerate(group):
            copies.append(pltpu.make_async_remote_copy(
                src_ref=source.at[to] if stage == 0 else source, dst_ref=target,
                send_sem=ask_send.at[stage, i], recv_sem=ask_recv.at[stage, i],
                device_id=peer, device_id_type=MESH,
            ))
            copies[-1].start()
        return copies

    asks = tell(0, group_1, requests, heard_1.at[me_1])
    for swap in swaps:
        swap.start()
    heard_1[me_1] = requests[me_1]

    landing = (o_2 * 8 + o_1) * 16 + slot
    columns = iota((BLOCK, CHIPS * 16), 1)
    for t in range(2):
        places[t * BLOCK:(t + 1) * BLOCK] = jnp.where(columns == landing + 8 * t, 1.0, 0.0).astype(BF16)

    for copy in asks:
        copy.wait_recv()
    later = tell(1, group_2, heard_1, heard_2.at[me_2])
    heard_2[me_2] = heard_1[...]
    lane = iota((CHIPS * SLOTS, 128), 1).astype(F32)

    def pick(heard, chips, target):
        heard = jnp.broadcast_to(heard.reshape(chips, 1, 128), (chips, SLOTS, 128))
        here = iota(heard.shape, 2) - iota(heard.shape, 1) == me_2 * SLOTS
        questions = jnp.sum(jnp.where(here, heard, 0.0), axis=2, keepdims=True).reshape(chips * SLOTS, 1)
        for j in range(2 * POOL_DEV // 128):
            hits = questions == lane[:chips * SLOTS] + 128.0 * j
            target[:, j * 128:(j + 1) * 128] = jnp.where(hits, 1.0, 0.0).astype(BF16)

    def found(picked, chips, first, width):
        rows = [dot(picked[...], pools[t, :, first:first + width]) for t in range(2)]
        return jnp.concatenate([r.reshape(chips, SLOTS, width) for r in rows], axis=1).astype(BF16)

    def answer(source, p, way, sem):
        return pltpu.make_async_remote_copy(
            src_ref=source, dst_ref=backs[p].at[chip], send_sem=sem, recv_sem=row_recv.at[p],
            device_id=device(way), device_id_type=MESH,
        )

    pick(heard_1[...], 8, early_picks)
    for copy in loads:
        copy.wait()
    for p, (first, width) in enumerate(PARTS):
        for swap in swaps[2 * p:2 * p + 2]:
            swap.wait_recv()
        early[p][...] = found(early_picks, 8, first, width)
        for way in NEAR:
            answer(early[p].at[first_half(way)], p, way, early_send.at[p]).start()
        backs[p][chip] = early[p][me_1]

    for copy in later:
        copy.wait_recv()
    asks = asks + later
    others = pl.ds(0, CHIPS - 1)
    far = pl.ds(0, len(FAR))
    near = pl.ds(0, len(NEAR))
    pick(heard_2[...], CHIPS, picks)
    for p, (first, width) in enumerate(PARTS):
        outs[p][...] = found(picks, CHIPS, first, width)
        for way in FAR:
            answer(outs[p].at[number(way)], p, way, row_send.at[p]).start()

    odd = lax.rem(a, 2)
    neighbour = (a + 1 - 2 * odd, c)
    rings = {}

    def ring(p, role, source, target, peer):
        span = pl.ds(PARTS[p][0], PARTS[p][1])
        rings[p, role] = pltpu.make_async_remote_copy(
            src_ref=source.at[:, span], dst_ref=target.at[:, span],
            send_sem=ring_send.at[p, role], recv_sem=ring_recv.at[p, role],
            device_id=peer, device_id_type=MESH,
        )
        rings[p, role].start()

    def own_block(t):
        return raw.at[pl.ds(pl.multiple_of(t * BLOCK, BLOCK), BLOCK)]

    def pass_on(p):
        rings[p, 0].wait_recv()
        ring(p, 3, others_in.at[1 - odd, 1], others_in.at[1 - odd, 0], neighbour)

    for p, (first, width) in enumerate(PARTS):
        pltpu.make_async_copy(backs[p].at[others], backs[p].at[others], row_recv.at[p]).wait()
        rows = dot(places[...], backs[p][...].reshape(CHIPS * 16, width))
        raw[:, first:first + width] = rows.astype(BF16)
        for role, t in ((0, 1 - odd), (1, odd)):
            ring(p, role, own_block(t), others_in.at[t, 1], (lax.rem(a + 2 + 28 * t, 32), c))
        ring(p, 2, own_block(odd), others_in.at[odd, 0], neighbour)
        if p >= LAG:
            pass_on(p - LAG)
    for p in range(len(PARTS) - LAG, len(PARTS) - 1):
        pass_on(p)

    def finish():
        for copy in asks:
            copy.wait_send()
        for p in range(len(PARTS)):
            pltpu.make_async_copy(outs[p].at[far], outs[p].at[far], row_send.at[p]).wait()
            pltpu.make_async_copy(early[p].at[near], early[p].at[near], early_send.at[p]).wait()
        for swap in swaps:
            swap.wait_send()
        for copy in rings.values():
            copy.wait_send()

    def normalized(block):
        rows = block.astype(F32)
        return (rows * lax.rsqrt(jnp.sum(rows * rows, axis=-1, keepdims=True) + norm_eps)).astype(BF16)

    def weights(left, right, positive):
        values = 1.0 / (1.0 + jnp.exp(-(logit_scale * dot_t(left, right) + logit_bias)))
        if positive:
            values = values - jnp.where(eye, 1.0, 0.0)
        return values.astype(BF16)

    for t in range(2):
        units[t] = normalized(raw[t * BLOCK:(t + 1) * BLOCK])
    for side in range(2):
        acc[side] = dot(weights(units[side], units[1 - side], True), units[1 - side])
    pass_on(len(PARTS) - 1)
    for role, t, k in ((0, 1 - odd, 2), (1, odd, 2), (2, 1 - odd, 1), (3, odd, 1)):
        if role:
            for p in range(len(PARTS)):
                rings[p, role].wait_recv()
        block = normalized(others_in[t, k - 1])
        acc[1 - t] += dot(weights(units[1 - t], block, False), block)
        if role == 2:
            for i in range(0, BLOCK, ROWS):
                span = pl.ds(i, ROWS)
                at = pl.ds(pl.multiple_of(odd * BLOCK + i, ROWS), ROWS)
                acc[odd, span] = unnormalized(raw[at], acc[odd, span])
    finish()


def write(total, raw, grad_text, grad_image, done, sem):
    odd = lax.rem(lax.axis_index("dp"), 2)
    targets = (grad_text, grad_image)
    for side in range(2):

        @pl.when(odd == side)
        def _():
            whole = pltpu.make_async_copy(total.at[side], targets[side], sem.at[0])
            whole.start()
            copies = [whole]
            for i in range(0, BLOCK, ROWS):
                span = pl.ds(i, ROWS)
                done[span] = unnormalized(raw[pl.ds((1 - side) * BLOCK + i, ROWS)], total[1 - side, span])
                copies.append(pltpu.make_async_copy(done.at[span], targets[1 - side].at[span], sem.at[1 + i // ROWS]))
                copies[-1].start()
            for copy in copies:
                copy.wait()


def shards(pool_image, pool_text, owners, slot_index):
    widths = [width for _, width in PARTS]
    hbm, vmem = pl.BlockSpec(memory_space=pltpu.HBM), pl.BlockSpec(memory_space=pltpu.VMEM)
    total, raw = pl.pallas_call(
        kernel,
        out_shape=(pltpu.VMEM((2, BLOCK, EMBED), F32), pltpu.VMEM((2 * BLOCK, EMBED), BF16)),
        in_specs=[hbm] * 4,
        out_specs=(vmem, vmem),
        scratch_shapes=[
            pltpu.VMEM((1, BLOCK), jnp.int32),
            pltpu.VMEM((1, BLOCK), jnp.int32),
            pltpu.VMEM((2, 2 * POOL_DEV, EMBED), BF16),
            pltpu.VMEM((8, 1, 128), F32),
            pltpu.VMEM((8, 1, 128), F32),
            pltpu.VMEM((8, 8, 1, 128), F32),
            pltpu.VMEM((8 * SLOTS, 2 * POOL_DEV), BF16),
            pltpu.VMEM((CHIPS * SLOTS, 2 * POOL_DEV), BF16),
            pltpu.VMEM((2 * BLOCK, CHIPS * 16), BF16),
            [pltpu.VMEM((8, 16, width), BF16) for width in widths],
            [pltpu.VMEM((CHIPS, 16, width), BF16) for width in widths],
            [pltpu.VMEM((CHIPS, 16, width), BF16) for width in widths],
            pltpu.VMEM((2, 2, BLOCK, EMBED), BF16),
            pltpu.VMEM((2, BLOCK, EMBED), BF16),
            pltpu.SemaphoreType.DMA((2,)),
            pltpu.SemaphoreType.DMA((2,)),
            pltpu.SemaphoreType.DMA((2, len(PARTS))),
            pltpu.SemaphoreType.DMA((2, len(PARTS))),
            pltpu.SemaphoreType.DMA((2, 7)),
            pltpu.SemaphoreType.DMA((2, 7)),
            pltpu.SemaphoreType.DMA((len(PARTS),)),
            pltpu.SemaphoreType.DMA((len(PARTS),)),
            pltpu.SemaphoreType.DMA((len(PARTS),)),
            pltpu.SemaphoreType.DMA((len(PARTS), 4)),
            pltpu.SemaphoreType.DMA((len(PARTS), 4)),
        ],
        compiler_params=pltpu.CompilerParams(
            collective_id=0, has_side_effects=True, vmem_limit_bytes=LIMIT_1 * 1024 * 1024
        ),
    )(*[
        pltpu.with_memory_space_constraint(operand, pltpu.HBM)
        for operand in (pool_image, pool_text, owners.reshape(1, BLOCK), slot_index.reshape(1, BLOCK))
    ])
    grad_text, grad_image = pl.pallas_call(
        write,
        out_shape=[jax.ShapeDtypeStruct((BLOCK, EMBED), F32)] * 2,
        in_specs=[vmem, vmem],
        out_specs=[pl.BlockSpec(memory_space=pltpu.HBM)] * 2,
        scratch_shapes=[
            pltpu.VMEM((BLOCK, EMBED), F32),
            pltpu.SemaphoreType.DMA((1 + BLOCK // ROWS,)),
        ],
        compiler_params=pltpu.CompilerParams(vmem_limit_bytes=LIMIT_2 * 1024 * 1024),
    )(total, raw)
    return grad_image, grad_text


def solution(mesh):
    in_specs = (
        P(("dp", "pool"), None),
        P(("dp", "pool"), None),
        P(("dp", "pool"), None),
        P(("dp", "pool")),
    )
    out_specs = (P(("dp", "pool"), None), P(("dp", "pool"), None))
    return jax.shard_map(shards, mesh=mesh, in_specs=in_specs, out_specs=out_specs, check_vma=False)
```
